32 devices in a mesh: batch: 8 (over z, x), head: 4 (over y, core).
Axes of the slice: x: 2, y: 2, z: 4, core: 2. Of those that a mesh axis runs over, the one named last changes fastest.
Arguments:
- tokens: bfloat16 [8192, 768], P('batch'), may hold values from -6 to 6
- lengths: int32 [16], P('batch'), may hold values from 64 to 512, as said below
- w_query: bfloat16 [768, 768], P(None, 'head'), may hold values from -0.21875 to 0.21875
- w_key: bfloat16 [768, 768], P(None, 'head'), may hold values from -0.21875 to 0.21875
- w_value: bfloat16 [768, 768], P(None, 'head'), may hold values from -0.21875 to 0.21875
- w_out: bfloat16 [768, 768], P('head'), may hold values from -1.75 to 1.75
- query_down_frozen: bfloat16 [768, 8], replicated, may hold values from -0.21875 to 0.21875
- value_down_frozen: bfloat16 [768, 8], replicated, may hold values from -0.21875 to 0.21875
- query_up_trained: bfloat16 [8, 768], P(None, 'head'), may hold values from -1 to 1
- value_up_trained: bfloat16 [8, 768], P(None, 'head'), may hold values from -1 to 1
- w_up: bfloat16 [768, 3072], P(None, 'head'), may hold values from -0.21875 to 0.21875
- w_down: bfloat16 [3072, 768], P('head'), may hold values from -0.109375 to 0.109375
- gain_attn: float32 [768], replicated, may hold values from 0.1 to 1.9
- gain_ffn: float32 [768], replicated, may hold values from 0.1 to 1.9
- cotangent: bfloat16 [8192, 768], P('batch'), may hold values from -6 to 6
Outputs:
- activations: bfloat16 [8192, 768], P('batch')
- input_grad: bfloat16 [8192, 768], P('batch')
- grad_b_query: float32 [8, 768], P(None, 'head')
- grad_b_value: float32 [8, 768], P(None, 'head')
The draws below stay inside these ranges and needn't reach their ends.
Inputs may be any that keep to these rules, and one draw needn't show every extreme that they name: `lengths`: some sequence has all 512 tokens in every draw.
All inputs are finite; a program needn't handle non-finite values.
Results may differ from the reference program's by a relative error of at most 0.018.
The reference program's roundings to bfloat16 on the way count: a program that leaves them out, or rounds other values in their place, can miss the bound.
Values may be sent and summed in bfloat16 or wider, within the bound.
A program may use at most 64 MiB of HBM per device.

```python
import jax
import jax.numpy as jnp
from jax import lax

D = 768
HD = 64
FF = 3072
RANK = 8
LMAX = 512
SEQS = 16
TOKENS = 8192


def draw_lengths(key, part):
    key = jax.random.fold_in(key, 7)
    first, second = jax.random.split(key)
    drawn_len = jax.random.randint(first, (SEQS,), LMAX // 8, LMAX + 1, dtype=jnp.int32)
    chosen = jax.random.randint(second, (), 0, SEQS, dtype=jnp.int32)
    return jnp.where(jnp.arange(SEQS, dtype=jnp.int32) == chosen, LMAX, drawn_len).astype(jnp.int32)


def steps_of(own_key, dims, cuts, low, top_value):
    level = 1.0
    for position, shards_of in cuts:
        steps = jax.random.uniform(jax.random.fold_in(jax.random.fold_in(own_key, 6), position), (shards_of,), jnp.float32, low / len(cuts), top_value / len(cuts))
        level = level * jnp.repeat(jnp.exp(steps), dims[position] // shards_of).reshape((-1,) + (1,) * (len(dims) - 1 - position))
    return level


def centred(rng, dims, deviation, bound, cuts=(), held_as=jnp.bfloat16):
    loudness = steps_of(rng, dims, cuts, -0.22, 0.18) if cuts else 1.0
    values = jax.random.normal(rng, dims, jnp.float32) * deviation * loudness
    return jnp.minimum(jnp.maximum(values, -bound), bound).astype(held_as)


def setup_inputs(seed: int = 0) -> dict:
    arg_keys = jax.random.split(jax.random.key(seed), 16)
    return {
        "tokens": centred(arg_keys[0], (TOKENS, D), 1.0, 6.0, ((0, 8),)),
        "lengths": draw_lengths(jax.random.fold_in(arg_keys[15], 71), 0),
        "w_query": centred(arg_keys[2], (D, D), D ** -0.5, 0.21875, ((1, 4),)),
        "w_key": centred(arg_keys[3], (D, D), D ** -0.5, 0.21875, ((1, 4),)),
        "w_value": centred(arg_keys[4], (D, D), D ** -0.5, 0.21875, ((1, 4),)),
        "w_out": centred(arg_keys[5], (D, D), (D // 64) ** -0.5, 1.75, ((0, 4),)),
        "query_down_frozen": centred(arg_keys[6], (D, RANK), D ** -0.5, 0.21875),
        "value_down_frozen": centred(arg_keys[7], (D, RANK), D ** -0.5, 0.21875),
        "query_up_trained": centred(arg_keys[8], (RANK, D), (4 * RANK) ** -0.5, 1.0, ((1, 4),)),
        "value_up_trained": centred(arg_keys[9], (RANK, D), (4 * RANK) ** -0.5, 1.0, ((1, 4),)),
        "w_up": centred(arg_keys[10], (D, FF), D ** -0.5, 0.21875, ((1, 4),)),
        "w_down": centred(arg_keys[11], (FF, D), FF ** -0.5, 0.109375, ((0, 4),)),
        "gain_attn": jnp.clip(1.0 + 0.18 * jax.random.normal(arg_keys[12], (D,), jnp.float32), 0.1, 1.9),
        "gain_ffn": jnp.clip(1.0 + 0.18 * jax.random.normal(arg_keys[13], (D,), jnp.float32), 0.1, 1.9),
        "cotangent": centred(arg_keys[14], (TOKENS, D), 1.0, 6.0, ((0, 8),)),
    }


@jax.custom_vjp
def low(v):
    return lax.optimization_barrier(v.astype(jnp.bfloat16)).astype(jnp.float32)

@jax.custom_vjp
def low_back(v):
    return v

def low_keep(v):
    return (low(v), None)

def low_pass(kept, grad):
    return (grad,)

def back_keep(v):
    return (v, None)

def back_low(kept, grad):
    return (low(grad),)
low.defvjp(low_keep, low_pass)
low_back.defvjp(back_keep, back_low)
EPS = 1e-05

def product(left, right):
    return jnp.dot(left, right, precision=lax.Precision.HIGHEST)

def layer_norm(value_in, gain_vec):
    centre = value_in - lax.optimization_barrier(jnp.mean(value_in, axis=-1, keepdims=True))
    variance = lax.optimization_barrier(jnp.mean(centre * centre, axis=-1, keepdims=True))
    return centre * lax.rsqrt(variance + EPS) * gain_vec

def attend_sequence(queries, key_rows, values, length):
    seq_len = queries.shape[0]
    head_count = queries.shape[1] // HD
    query_heads = queries.reshape(seq_len, head_count, HD)
    key_heads = key_rows.reshape(seq_len, head_count, HD)
    value_heads = values.reshape(seq_len, head_count, HD)
    scores = jnp.einsum('qhd,khd->hqk', query_heads, key_heads, precision=lax.Precision.HIGHEST) * 0.125
    key_keep = jnp.arange(seq_len, dtype=jnp.int32) < length
    scores = jnp.where(key_keep[None, None, :], scores, -1e+30)
    scores = low_back(scores)
    probability = low(jax.nn.softmax(scores, axis=-1))
    context = jnp.einsum('hqk,khd->qhd', probability, value_heads, precision=lax.Precision.HIGHEST)
    return context.reshape(seq_len, head_count * HD)

def reference(tokens, lengths, w_query, w_key, w_value, w_out, query_down_frozen, value_down_frozen, query_up_trained, value_up_trained, w_up, w_down, gain_attn, gain_ffn, cotangent):
    single_float = jnp.float32
    inputs = tokens.astype(single_float)
    wq, wk, wv, wo = (w_query.astype(single_float), w_key.astype(single_float), w_value.astype(single_float), w_out.astype(single_float))
    aq, av = (query_down_frozen.astype(single_float), value_down_frozen.astype(single_float))
    w_one, w_two = (w_up.astype(single_float), w_down.astype(single_float))
    gain_one, gain_two = (gain_attn.astype(single_float), gain_ffn.astype(single_float))
    valid = (jnp.arange(LMAX, dtype=jnp.int32)[None, :] < lengths[:, None]).astype(single_float).reshape(TOKENS, 1)
    attend_ckpt = jax.checkpoint(attend_sequence)

    def forward(x_full, bq_full, bv_full):
        low_q = low(product(x_full, aq))
        low_v = low(product(x_full, av))
        queries = low_back(low(product(x_full, wq) + 2.0 * product(low_q, bq_full)))
        key_rows = low_back(low(product(x_full, wk)))
        values = low_back(low(product(x_full, wv) + 2.0 * product(low_v, bv_full)))
        packed_in = (queries.reshape(SEQS, LMAX, D), key_rows.reshape(SEQS, LMAX, D), values.reshape(SEQS, LMAX, D), lengths)
        context = lax.map(lambda packed: attend_ckpt(*packed), packed_in).reshape(TOKENS, D)
        context = low_back(low(context))
        attn = low_back(product(context, wo))
        hidden_one = layer_norm(x_full + attn, gain_one)
        up_pre = low_back(product(low(hidden_one), w_one))
        act = low(jax.nn.gelu(up_pre, approximate=False))
        ffn = low_back(product(act, w_two))
        return valid * layer_norm(hidden_one + ffn, gain_two)
    result, pull = jax.vjp(forward, inputs, query_up_trained.astype(single_float), value_up_trained.astype(single_float))
    grad_inputs, grad_bq, grad_bv = pull(cotangent.astype(single_float))
    return (result.astype(jnp.bfloat16), grad_inputs.astype(jnp.bfloat16), grad_bq, grad_bv)
```

```python
import functools

import jax
import jax.numpy as jnp
from jax import lax
from jax.experimental import pallas as pl
from jax.experimental.pallas import tpu as pltpu
from jax.sharding import PartitionSpec as P

HD = 64
BF16 = jnp.bfloat16
F32 = jnp.float32
MESH = pl.DeviceIdType.MESH

OUT, UP, DOWN, QKV = 0, 1, 5, 9
STAGES = ((0, 1), (1, 2), (3, 2), (5, 2), (7, 2), (9, 3))
OWN, SIB, FAR, FARSIB = 0, 1, 2, 3
INPUT_CHUNKS = 4


def dot(left, right, left_dim=1, right_dim=0):
    return lax.dot_general(
        left, right, (((left_dim,), (right_dim,)), ((), ())), preferred_element_type=F32
    )


def norm(z):
    centre = z - jnp.mean(z, axis=-1, keepdims=True)
    inverse = lax.rsqrt(jnp.mean(centre * centre, axis=-1, keepdims=True) + 1e-05)
    return centre * inverse, inverse


def norm_back(scaled, normed, inverse):
    return inverse * (
        scaled
        - jnp.mean(scaled, axis=-1, keepdims=True)
        - normed * jnp.mean(scaled * normed, axis=-1, keepdims=True)
    )


def flip(index, bit):
    return index + bit - 2 * bit * ((index // bit) % 2)


def kernel(
    batch_steps,
    lengths,
    tokens,
    w_query,
    w_key,
    w_value,
    w_out,
    w_up,
    w_down,
    down_query,
    down_value,
    up_query,
    up_value,
    gain_one,
    gain_two,
    cotangent,
    activations,
    input_grad,
    grad_adapters,
    x,
    raw,
    w,
    raw_down,
    raw_up,
    gains,
    cot,
    adapter_down,
    adapter_up,
    low,
    q,
    k,
    v,
    probs,
    ctx_out,
    ctx_in,
    normed_one,
    inverse_one,
    hidden,
    hidden_low,
    act,
    slope,
    total,
    grad_z2,
    grad_low,
    grad_z1,
    dctx_out,
    dctx_in,
    dq,
    dk,
    dv,
    part_out,
    part_in,
    rows_out,
    grads,
    grads_in,
    local_sem,
    send_sem,
    recv_sem,
):
    b = lax.axis_index("batch")
    h = lax.axis_index("head")
    core = h % 2
    seq = h // 2
    far_seq = 1 - seq
    part = b % 4
    sibling = (b, flip(h, 1))
    across = (b, flip(h, 2))
    diagonal = (b, 3 - h)
    x_peer = (flip(b, 1), h)
    z_peer = (flip(b, 2), h)
    batch_peers = [(flip(b, 1 << s), h) for s in range(batch_steps)]

    numbers = {}
    started = []
    local_numbers = {}

    def number(key):
        return numbers.setdefault(key, len(numbers))

    def copy(key, source, target, device):
        n = number(key)
        return pltpu.make_async_remote_copy(
            src_ref=source,
            dst_ref=target,
            send_sem=send_sem.at[n],
            recv_sem=recv_sem.at[n],
            device_id=device,
            device_id_type=MESH,
        )

    def send(key, source, target, device):
        c = copy(key, source, target, device)
        c.start()
        started.append(c)

    def arrived(key, target, device=None):
        copy(key, target, target, sibling).wait_recv()

    def load(key, source, target):
        c = pltpu.make_async_copy(
            source, target, local_sem.at[local_numbers.setdefault(key, len(local_numbers))]
        )
        c.start()
        return c

    raw_loads = [load(f"w{j}", r, raw.at[j]) for j, r in enumerate((w_query, w_key, w_value))]
    x_far_load = load("xf", tokens.at[pl.ds(2 * far_seq, 2)], x.at[pl.ds(2 * far_seq, 2)])
    small_loads = [
        load("s0", down_query, raw_down.at[0]),
        load("s1", down_value, raw_down.at[1]),
        load("s2", up_query, raw_up.at[0]),
        load("s3", up_value, raw_up.at[1]),
    ]
    x_own_load = load("xo", tokens.at[pl.ds(2 * seq, 2)], x.at[pl.ds(2 * seq, 2)])
    out_load = load("wo", w_out, w.at[OWN, pl.ds(OUT, 1)])
    up_load = load("wu", w_up, w.at[OWN, pl.ds(UP, 4)])
    down_load = load("wd", w_down, w.at[OWN, pl.ds(DOWN, 4)])
    late_loads = [
        load("g1", gain_one, gains.at[0]),
        load("g2", gain_two, gains.at[1]),
        load("co", cotangent.at[h], cot),
    ]

    barrier = pltpu.get_barrier_semaphore()
    peers = [sibling, across, diagonal] + batch_peers
    for peer in peers:
        pl.semaphore_signal(barrier, inc=1, device_id=peer, device_id_type=MESH)
    pl.semaphore_wait(barrier, len(peers))

    def rows_of(ref, first, count, index, third=None):
        if third is None:
            return ref.at[pl.ds(first, count), pl.ds(pl.multiple_of(48 * index, 16), 48)]
        return ref.at[pl.ds(first, count), pl.ds(pl.multiple_of(48 * index + 16 * third, 16), 16)]

    far = w.at[FAR]
    px, pz, pd = flip(part, 1), flip(part, 2), 3 - part

    def relay_start(s):
        if s >= len(STAGES):
            return
        first, count = STAGES[s]
        if first >= QKV:
            source, at = w.at[OWN], first
        elif first >= DOWN:
            source, at = w_down, first - DOWN
        elif first >= UP:
            source, at = w_up, first - UP
        else:
            source, at = w_out, first
        send(("y", s), rows_of(source, at, count, part), rows_of(far, first, count, part), across)
        send(
            ("y3", s),
            rows_of(source, at, count, pd, 0),
            rows_of(far, first, count, pd, 0),
            across,
        )

    def relay_one(s):
        first, count = STAGES[s]
        mine = rows_of(far, first, count, part)
        arrived(("y", s), mine)
        send(("x", s), mine, mine, x_peer)
        send(("z", s), mine, mine, z_peer)
        relay_start(s + 2)

    def relay_two(s):
        first, count = STAGES[s]
        arrived(("x", s), rows_of(far, first, count, px))
        piece = rows_of(far, first, count, px, 2)
        send(("z3", s), piece, piece, z_peer)
        arrived(("z", s), rows_of(far, first, count, pz))
        piece = rows_of(far, first, count, pz, 1)
        send(("x3", s), piece, piece, x_peer)

    def relay_three(s):
        first, count = STAGES[s]
        arrived(("y3", s), rows_of(far, first, count, pd, 0))
        arrived(("x3", s), rows_of(far, first, count, pd, 1))
        arrived(("z3", s), rows_of(far, first, count, pd, 2))
        if first < QKV:
            items = pl.ds(first, count)
            send(("c", s), w.at[FAR, items], w.at[FARSIB, items], sibling)

    def relay_end(s):
        first, count = STAGES[s]
        arrived(("c", s), w.at[FARSIB, pl.ds(first, count)])

    relay_start(0)
    relay_start(1)
    send("so", w_out, w.at[SIB, pl.ds(OUT, 1)], sibling)
    send("su", w_up, w.at[SIB, pl.ds(UP, 4)], sibling)
    send("sd", w_down, w.at[SIB, pl.ds(DOWN, 4)], sibling)

    for c in small_loads:
        c.wait()
    adapter_down[...] = jnp.concatenate([raw_down[0], raw_down[1]] * 2, axis=1)
    nothing = jnp.zeros((8, 192), F32)
    adapter_up[0, 0] = jnp.concatenate([raw_up[0].astype(F32), nothing], axis=0)
    adapter_up[0, 1] = jnp.concatenate([nothing, raw_up[1].astype(F32)], axis=0)
    send("b", adapter_up.at[0], adapter_up.at[1], across)

    for j in range(3):
        raw_loads[j].wait()
        w[OWN, QKV + j] = raw[j].T

    def project(rows, which, slot, store):
        xs = x[pl.ds(2 * rows, 2)].reshape(512, 768)
        lows = dot(xs, adapter_down[:, :16]).astype(BF16)
        ups = adapter_up[0 if slot == OWN else 1].astype(BF16)
        if store:
            low[...] = lows
        for ref, j in ((q, 0), (k, 1), (v, 2)):
            full = dot(xs, w[slot, QKV + j], 1, 1)
            if j != 1:
                full = full + 2.0 * dot(lows, ups[j // 2])
            full = full.astype(BF16)
            for head in range(3):
                ref[which, head] = full[:, head * HD : (head + 1) * HD]

    def attend(rows, which, context):
        keep = lax.broadcasted_iota(jnp.int32, (512, 1), 0) < lengths[rows]
        for head in range(3):
            scores = jnp.where(keep, dot(k[which, head], q[which, head], 1, 1) * 0.125, -1e30)
            exponent = jnp.exp(scores - jnp.max(scores, axis=0, keepdims=True))
            weights = exponent * (1.0 / jnp.sum(exponent, axis=0, keepdims=True))
            weights = weights.astype(BF16)
            probs[which, head] = weights
            if context is not None:
                out = dot(v[which, head], weights, 0, 0).astype(BF16)
                columns = slice(head * HD, (head + 1) * HD)
                ctx_out[context, 0, columns] = out[:, :256]
                ctx_out[context, 1, columns] = out[:, 256:]

    x_far_load.wait()
    project(far_seq, 1, OWN, False)
    relay_one(0)
    attend(far_seq, 1, 1)
    send("cy", ctx_out.at[1, core], ctx_in.at[FAR], across)
    send("cd", ctx_out.at[1, 1 - core], ctx_in.at[FARSIB], diagonal)
    relay_one(1)
    relay_two(0)
    x_own_load.wait()
    project(seq, 0, OWN, True)
    relay_three(0)
    attend(seq, 0, 0)
    send("cc", ctx_out.at[0, 1 - core], ctx_in.at[SIB], sibling)
    ctx_in[OWN] = ctx_out[0, core]
    relay_one(2)
    relay_two(1)

    out_load.wait()
    for c in late_loads:
        c.wait()
    arrived("so", w.at[SIB, pl.ds(OUT, 1)])
    relay_end(0)
    arrived("cc", ctx_in.at[SIB])
    arrived("cy", ctx_in.at[FAR])
    arrived("cd", ctx_in.at[FARSIB])
    all_out = w[:, OUT].reshape(768, 768)
    attn = dot(ctx_in[...].reshape(768, 256), all_out, 0, 0)
    n1, r1 = norm(x[h].astype(F32) + attn)
    normed_one[...] = n1
    inverse_one[...] = r1
    h1 = n1 * gains[0]
    hidden[...] = h1
    hidden_low[...] = h1.astype(BF16)

    def go_up(slot):
        up = dot(hidden_low[...], w[slot, UP : UP + 4].reshape(768, 768))
        phi = 0.5 * (1.0 + lax.erf(up * 0.7071067811865476))
        slope[slot] = phi + up * (0.3989422804014327 * jnp.exp(-0.5 * up * up))
        act[slot] = (up * phi).astype(BF16)

    def go_down(slot):
        return dot(act[slot], w[slot, DOWN : DOWN + 4].reshape(768, 768))

    up_load.wait()
    down_load.wait()
    go_up(OWN)
    total[...] = hidden[...] + go_down(OWN)
    relay_three(1)
    arrived("su", w.at[SIB, pl.ds(UP, 4)])
    arrived("sd", w.at[SIB, pl.ds(DOWN, 4)])
    go_up(SIB)
    total[...] += go_down(SIB)
    relay_one(3)
    relay_two(2)
    relay_three(2)
    go_up(FAR)
    relay_one(4)
    relay_two(3)
    relay_end(1)
    relay_end(2)
    go_up(FARSIB)
    relay_three(3)
    relay_one(5)
    relay_two(4)
    relay_three(4)
    total[...] += go_down(FAR)
    relay_end(3)
    relay_end(4)
    z2 = total[...] + go_down(FARSIB)

    n2, r2 = norm(z2)
    position = lax.broadcasted_iota(jnp.int32, (256, 1), 0) + 256 * core
    valid = (position < lengths[seq]).astype(F32)
    rows_out[0] = (valid * (n2 * gains[1])).astype(BF16)
    send("ay", rows_out.at[0], activations.at[h], across)
    send("ac", rows_out.at[0], activations.at[h], sibling)
    act_store = load("a", rows_out.at[0], activations.at[h])
    d_z2 = norm_back(cot[...].astype(F32) * valid * gains[1], n2, r2)
    grad_low[...] = d_z2.astype(BF16)
    grad_z2[...] = d_z2

    def back(slot):
        d_act = dot(grad_low[...], w[slot, DOWN : DOWN + 4].reshape(768, 768), 1, 1)
        d_up = (d_act * slope[slot]).astype(BF16)
        grad_z2[...] += dot(d_up, w[slot, UP : UP + 4].reshape(768, 768), 1, 1)

    back(OWN)
    back(SIB)
    relay_two(5)
    back(FAR)
    back(FARSIB)

    d_z1 = norm_back(grad_z2[...] * gains[0], normed_one[...], inverse_one[...])
    grad_z1[...] = d_z1
    all_out = w[:, OUT].reshape(768, 768)
    d_ctx = dot(all_out, d_z1.astype(BF16), 1, 1).astype(BF16)
    dctx_out[...] = d_ctx.reshape(4, 192, 256)
    send("d0", dctx_out.at[SIB], dctx_in.at[0, core], sibling)
    send("d1", dctx_out.at[FARSIB], dctx_in.at[1, core], sibling)
    dctx_in[0, core] = dctx_out[OWN]
    dctx_in[1, core] = dctx_out[FAR]

    relay_three(5)
    arrived("b", adapter_up.at[1])
    project(seq, 1, FAR, False)
    attend(seq, 1, None)
    arrived("ay", activations.at[flip(h, 2)])
    send("ar", activations.at[flip(h, 2)], activations.at[flip(h, 2)], sibling)
    arrived("d0", dctx_in.at[0, 1 - core])
    arrived("d1", dctx_in.at[1, 1 - core])

    def attend_back(which):
        for head in range(3):
            columns = slice(head * HD, (head + 1) * HD)
            d_out = jnp.concatenate(
                [dctx_in[which, 0, columns], dctx_in[which, 1, columns]], axis=1
            )
            weights = probs[which, head]
            probability = weights.astype(F32)
            d_weights = dot(v[which, head], d_out)
            mean = jnp.sum(probability * d_weights, axis=0, keepdims=True)
            d_scores = (probability * (d_weights - mean)).astype(BF16)
            d_value = dot(weights, d_out, 1, 1).astype(BF16)
            d_key = (0.125 * dot(d_scores, q[which, head])).astype(BF16)
            d_query = (0.125 * dot(k[which, head], d_scores, 0, 0)).astype(BF16)
            for half in range(2):
                span = slice(256 * half, 256 * half + 256)
                dv[which, half, :, columns] = d_value[span]
                dk[which, half, :, columns] = d_key[span]
                dq[which, half, columns] = d_query[:, span]

    attend_back(0)
    attend_back(1)

    lows = low[...].reshape(2, 256, 16)

    def adapter_grads(which):
        return [
            2.0
            * (
                dot(lows[0], dq[which, 0], 0, 1) + dot(lows[1], dq[which, 1], 0, 1)
                if j == 0
                else dot(lows[0], dv[which, 0], 0, 0) + dot(lows[1], dv[which, 1], 0, 0)
            )
            for j in range(2)
        ]

    def input_part(half):
        part_sum = 0.0
        d_low = 0.0
        for which, slot in ((0, OWN), (1, FAR)):
            part_sum = part_sum + dot(dq[which, half], w[slot, QKV], 0, 0)
            part_sum = part_sum + dot(dk[which, half], w[slot, QKV + 1])
            part_sum = part_sum + dot(dv[which, half], w[slot, QKV + 2])
            ups = adapter_up[which].astype(BF16)
            d_low = d_low + dot(dq[which, half], ups[0], 0, 1) + dot(dv[which, half], ups[1], 1, 1)
        d_low = 2.0 * d_low
        coarse = d_low.astype(BF16)
        fine = (d_low - coarse.astype(F32)).astype(BF16)
        both = jnp.concatenate([coarse, fine], axis=1)
        return part_sum + dot(both, adapter_down[...], 1, 1)

    part_out[...] = input_part(1 - core).astype(BF16)
    send("p", part_out, part_in, sibling)
    grad_z1[...] += input_part(core)
    arrived("p", part_in)
    span = 256 // INPUT_CHUNKS
    for t in range(INPUT_CHUNKS):
        rows = pl.ds(span * t, span)
        rows_out[1, rows] = (grad_z1[rows] + part_in[rows].astype(F32)).astype(BF16)
        send(("iy", t), rows_out.at[1, rows], input_grad.at[h, rows], across)
    send("ic", rows_out.at[1], input_grad.at[h], sibling)
    grad_store = load("i", rows_out.at[1], input_grad.at[h])

    for which in range(2):
        for j, term in enumerate(adapter_grads(which)):
            grads[which, j] = term
    send("g", grads.at[1], grads_in.at[0], across)
    arrived("g", grads_in.at[0])
    grads[0] += grads_in[0]
    for s in range(batch_steps):
        source = 0 if s == 0 else 1 + s
        send(("g", s), grads.at[source], grads_in.at[1 + s], batch_peers[s])
        arrived(("g", s), grads_in.at[1 + s])
        grads[2 + s] = grads[source] + grads_in[1 + s]
    final = grads[1 + batch_steps]
    grad_adapters[0] = final[0, 0:8]
    grad_adapters[1] = final[1, 8:16]

    for t in range(INPUT_CHUNKS):
        rows = pl.ds(span * t, span)
        block = input_grad.at[flip(h, 2), rows]
        arrived(("iy", t), block)
        send(("ir", t), block, block, sibling)
    arrived("ac", activations.at[flip(h, 1)])
    arrived("ar", activations.at[3 - h])
    arrived("ic", input_grad.at[flip(h, 1)])
    for t in range(INPUT_CHUNKS):
        arrived(("ir", t), input_grad.at[3 - h, pl.ds(span * t, span)])
    act_store.wait()
    grad_store.wait()
    for c in started:
        c.wait_send()


def body(batch_steps, *given):
    (
        tokens,
        lengths,
        w_query,
        w_key,
        w_value,
        w_out,
        down_query,
        down_value,
        up_query,
        up_value,
        w_up,
        w_down,
        gain_attn,
        gain_ffn,
        cotangent,
    ) = given
    anywhere = pl.BlockSpec(memory_space=pl.ANY)
    vmem = pltpu.VMEM
    activations, input_grad, grad_adapters = pl.pallas_call(
        functools.partial(kernel, batch_steps),
        out_shape=(
            jax.ShapeDtypeStruct((4, 256, 768), BF16),
            jax.ShapeDtypeStruct((4, 256, 768), BF16),
            jax.ShapeDtypeStruct((2, 8, 192), F32),
        ),
        in_specs=[pl.BlockSpec(memory_space=pltpu.SMEM)] + [anywhere] * 14,
        out_specs=(anywhere, anywhere, pl.BlockSpec(memory_space=pltpu.VMEM)),
        scratch_shapes=[
            vmem((4, 256, 768), BF16),
            vmem((3, 768, 192), BF16),
            vmem((4, 12, 192, 768), BF16),
            vmem((2, 768, 8), BF16),
            vmem((2, 8, 192), BF16),
            vmem((2, 1, 768), F32),
            vmem((256, 768), BF16),
            vmem((768, 32), BF16),
            vmem((2, 2, 16, 192), F32),
            vmem((512, 16), BF16),
            vmem((2, 3, 512, 64), BF16),
            vmem((2, 3, 512, 64), BF16),
            vmem((2, 3, 512, 64), BF16),
            vmem((2, 3, 512, 512), BF16),
            vmem((2, 2, 192, 256), BF16),
            vmem((4, 192, 256), BF16),
            vmem((256, 768), F32),
            vmem((256, 1), F32),
            vmem((256, 768), F32),
            vmem((256, 768), BF16),
            vmem((4, 256, 768), BF16),
            vmem((4, 256, 768), F32),
            vmem((256, 768), F32),
            vmem((256, 768), F32),
            vmem((256, 768), BF16),
            vmem((256, 768), F32),
            vmem((4, 192, 256), BF16),
            vmem((2, 2, 192, 256), BF16),
            vmem((2, 2, 192, 256), BF16),
            vmem((2, 2, 256, 192), BF16),
            vmem((2, 2, 256, 192), BF16),
            vmem((256, 768), BF16),
            vmem((256, 768), BF16),
            vmem((2, 256, 768), BF16),
            vmem((2 + batch_steps, 2, 16, 192), F32),
            vmem((1 + batch_steps, 2, 16, 192), F32),
            pltpu.SemaphoreType.DMA((20,)),
            pltpu.SemaphoreType.DMA((80,)),
            pltpu.SemaphoreType.DMA((80,)),
        ],
        compiler_params=pltpu.CompilerParams(
            collective_id=0, has_side_effects=True, vmem_limit_bytes=60 * 1024 * 1024
        ),
        cost_estimate=pl.CostEstimate(
            flops=11_000_000_000, bytes_accessed=20_000_000, transcendentals=4_000_000
        ),
    )(
        lengths,
        tokens.reshape(4, 256, 768),
        w_query,
        w_key,
        w_value,
        w_out.reshape(1, 192, 768),
        w_up.reshape(4, 192, 768),
        w_down.reshape(4, 192, 768),
        down_query,
        down_value,
        up_query,
        up_value,
        gain_attn.reshape(1, 768),
        gain_ffn.reshape(1, 768),
        cotangent.reshape(4, 256, 768),
    )
    return (
        activations.reshape(tokens.shape),
        input_grad.reshape(tokens.shape),
        grad_adapters[0],
        grad_adapters[1],
    )


def solution(mesh):
    batch_steps = mesh.shape["batch"].bit_length() - 1
    in_specs = (
        P("batch", None),
        P("batch"),
        P(None, "head"),
        P(None, "head"),
        P(None, "head"),
        P("head", None),
        P(),
        P(),
        P(None, "head"),
        P(None, "head"),
        P(None, "head"),
        P("head", None),
        P(),
        P(),
        P("batch", None),
    )
    out_specs = (P("batch", None), P("batch", None), P(None, "head"), P(None, "head"))
    return jax.shard_map(
        functools.partial(body, batch_steps),
        mesh=mesh,
        in_specs=in_specs,
        out_specs=out_specs,
        check_vma=False,
    )
```

```python
import functools

import jax
import jax.numpy as jnp
from jax import lax
from jax.experimental import pallas as pl
from jax.experimental.pallas import tpu as pltpu
from jax.sharding import PartitionSpec as P

HD = 64
BF16 = jnp.bfloat16
F32 = jnp.float32
MESH = pl.DeviceIdType.MESH

OUT, UP, DOWN, QKV, ADAPTER = 0, 1, 5, 9, 12
OWN, SIB, FAR, FARSIB = 0, 1, 2, 3
OVER_Y = (32, 16) * 6
GROUPS = ((0, 1), (1, 4), (5, 2), (7, 2), (9, 3))
CHUNKS = ((0, 128), (128, 64), (192, 64))
SEND_GROUPS = ("y", "x", "z", "t", "d", "c", "w", "ctx", "dctx", "rows", "b", "g")


def dot(left, right, left_dim=1, right_dim=0):
    return lax.dot_general(
        left, right, (((left_dim,), (right_dim,)), ((), ())), preferred_element_type=F32
    )


def norm(z):
    centre = z - jnp.mean(z, axis=-1, keepdims=True)
    inverse = lax.rsqrt(jnp.mean(centre * centre, axis=-1, keepdims=True) + 1e-05)
    return centre * inverse, inverse


def norm_back(scaled, normed, inverse):
    return inverse * (
        scaled
        - jnp.mean(scaled, axis=-1, keepdims=True)
        - normed * jnp.mean(scaled * normed, axis=-1, keepdims=True)
    )


def flip(index, bit):
    return index + bit - 2 * bit * ((index // bit) % 2)


def kernel(
    batch_steps,
    lengths,
    tokens,
    w_query,
    w_key,
    w_value,
    w_out,
    w_up,
    w_down,
    down_query,
    down_value,
    up_query,
    up_value,
    gain_one,
    gain_two,
    cotangent,
    activations,
    input_grad,
    grads_out,
    x,
    w,
    raw_down,
    raw_up,
    gains,
    cot,
    adapter_up,
    low,
    qkv,
    probs,
    ctx_out,
    ctx_in,
    normed_one,
    inverse_one,
    hidden,
    hidden_low,
    act,
    slope,
    total,
    grad_z1,
    dctx_out,
    dctx_in,
    grad_qkv,
    part_out,
    part_in,
    grads,
    grads_in,
    local_sem,
    send_sem,
    recv_sem,
):
    b = lax.axis_index("batch")
    h = lax.axis_index("head")
    core = h % 2
    seq = h // 2
    far_seq = 1 - seq
    part = b % 4
    sibling = (b, flip(h, 1))
    across = (b, flip(h, 2))
    diagonal = (b, 3 - h)
    x_peer = (flip(b, 1), h)
    z_peer = (flip(b, 2), h)
    xz_peer = (flip(flip(b, 1), 2), h)
    batch_peers = [(flip(b, 1 << s), h) for s in range(batch_steps)]

    barrier = pltpu.get_barrier_semaphore()
    peers = [sibling, across, diagonal, xz_peer] + batch_peers
    for peer in peers:
        pl.semaphore_signal(barrier, inc=1, device_id=peer, device_id_type=MESH)

    recv_numbers = {}
    local_numbers = {}

    def copy(group, key, source, target, device):
        number = recv_numbers.setdefault(key, len(recv_numbers))
        return pltpu.make_async_remote_copy(
            src_ref=source,
            dst_ref=target,
            send_sem=send_sem.at[SEND_GROUPS.index(group)],
            recv_sem=recv_sem.at[number],
            device_id=device,
            device_id_type=MESH,
        )

    def send(group, key, source, target, device):
        copy(group, key, source, target, device).start()

    def arrived(key, target):
        copy("y", key, target, target, sibling).wait_recv()

    def sent(group, ref):
        copy(group, ("y", 0), ref, ref, sibling).wait_send()

    def local(key, source, target):
        number = local_numbers.setdefault(key, len(local_numbers))
        return pltpu.make_async_copy(source, target, local_sem.at[number])

    def load(key, source, target):
        local(key, source, target).start()

    def loaded(key, target):
        local(key, target, target).wait()

    for j, ref in enumerate((w_query, w_key, w_value)):
        load("qkv", ref, w.at[OWN, QKV + j])
    load("far", tokens.at[pl.ds(2 * far_seq, 2)], x.at[pl.ds(2 * far_seq, 2)])
    load("downs", down_query, raw_down.at[0])
    load("downs", down_value, raw_down.at[1])
    load("ups", up_query, raw_up.at[0])
    load("ups", up_value, raw_up.at[1])
    load("own", tokens.at[pl.ds(2 * seq, 2)], x.at[pl.ds(2 * seq, 2)])
    load("w", w_out, w.at[OWN, pl.ds(OUT, 1)])
    load("w", w_up, w.at[OWN, pl.ds(UP, 4)])
    load("w", w_down, w.at[OWN, pl.ds(DOWN, 4)])
    load("one", gain_one, gains.at[0])
    load("two", gain_two, gains.at[1])
    load("cot", cotangent.at[h], cot)

    far = w.at[FAR]
    pd = 3 - part
    group_of = {}
    for first, count in GROUPS:
        for item in range(first, first + count):
            group_of[item] = first

    def rows_of(ref, item, index, start=0, count=48):
        return ref.at[item, pl.ds(pl.multiple_of(48 * index + start, 16), count)]

    def source_of(item):
        if item >= QKV:
            return w.at[OWN], item
        if item >= DOWN:
            return w_down, item - DOWN
        if item >= UP:
            return w_up, item - UP
        return w_out, item

    def send_part(*items):
        for item in items:
            source, at = source_of(item)
            mine, theirs = rows_of(source, at, part), rows_of(far, item, part)
            send("y", ("y", item), mine, theirs, across)

    def send_rest(*items):
        for item in items:
            source, at = source_of(item)
            count = OVER_Y[item]
            mine, theirs = rows_of(source, at, pd, 0, count), rows_of(far, item, pd, 0, count)
            send("t", ("f", group_of[item]), mine, theirs, across)

    def relay(*items):
        for item in items:
            mine = rows_of(far, item, part)
            arrived(("y", item), mine)
            key = ("f", group_of[item])
            send("x", key, mine, mine, x_peer)
            send("z", key, mine, mine, z_peer)
            count = OVER_Y[item]
            rest = rows_of(far, item, part, count, 48 - count)
            send("d", key, rest, rest, xz_peer)

    def collect(group):
        first, count = GROUPS[group]
        items = pl.ds(first, count)
        arrived(("f", first), w.at[FAR, items, pl.ds(0, 144)])
        if first < QKV:
            send("c", ("c", first), w.at[FAR, items], w.at[FARSIB, items], sibling)

    def collect_sibling(group):
        first, count = GROUPS[group]
        arrived(("c", first), w.at[FARSIB, pl.ds(first, count)])

    pl.semaphore_wait(barrier, len(peers))
    send_part(0, 1)
    send_rest(0)
    send_part(2, 3, 4, 5)
    send("w", "so", w_out, w.at[SIB, pl.ds(OUT, 1)], sibling)
    send("w", "su", w_up, w.at[SIB, pl.ds(UP, 4)], sibling)
    send("w", "sd", w_down, w.at[SIB, pl.ds(DOWN, 4)], sibling)

    loaded("downs", raw_down)
    loaded("ups", raw_up)
    downs = jnp.concatenate([raw_down[0].astype(F32), raw_down[1].astype(F32)] * 2, axis=0)
    w[OWN, ADAPTER, :32] = downs.astype(BF16)
    w[FAR, ADAPTER, :32] = downs.astype(BF16)
    nothing = jnp.zeros((8, 192), F32)
    adapter_up[0, :, :192] = jnp.concatenate([raw_up[0].astype(F32), nothing], axis=0)
    adapter_up[0, :, 192:384] = jnp.zeros((16, 192), F32)
    adapter_up[0, :, 384:] = jnp.concatenate([nothing, raw_up[1].astype(F32)], axis=0)
    send("b", "b", adapter_up.at[0], adapter_up.at[1], across)

    def adapted(slot, count):
        return w[slot, QKV:].reshape(768, 768)[:count]

    def project(rows, which, slot, store):
        full = dot(adapted(slot, 592), x[pl.ds(2 * rows, 2)].reshape(512, 768), 1, 1)
        lows = full[576:].astype(BF16)
        ups = adapter_up[0 if slot == OWN else 1].astype(BF16)
        if store:
            low[...] = lows
        query = full[:192] + 2.0 * dot(ups[:, :192], lows, 0, 0)
        value = full[384:576] + 2.0 * dot(ups[:, 384:], lows, 0, 0)
        qkv[which, :192] = query.astype(BF16)
        qkv[which, 192:384] = full[192:384].astype(BF16)
        qkv[which, 384:] = value.astype(BF16)

    def head_rows(j, head):
        return slice(192 * j + HD * head, 192 * j + HD * (head + 1))

    def attend(rows, which, context):
        position = lax.broadcasted_iota(jnp.int32, (512, 1), 0)
        bias = jnp.where(position < lengths[rows], 0.0, -1e30)
        for head in range(3):
            query = qkv[which, head_rows(0, head)] * jnp.asarray(0.125, BF16)
            scores = dot(qkv[which, head_rows(1, head)], query, 0, 0) + bias
            exponent = jnp.exp(scores - jnp.max(scores, axis=0, keepdims=True))
            weights = exponent * (1.0 / jnp.sum(exponent, axis=0, keepdims=True))
            probs[which, head] = weights.astype(BF16)
        if context is None:
            return
        for head in range(3):
            out = dot(qkv[which, head_rows(2, head)], probs[which, head]).astype(BF16)
            ctx_out[context, 0, head_rows(0, head)] = out[:, :256]
            ctx_out[context, 1, head_rows(0, head)] = out[:, 256:]

    loaded("qkv", w.at[OWN, pl.ds(QKV, 3)])
    loaded("far", x.at[pl.ds(2 * far_seq, 2)])
    project(far_seq, 1, OWN, False)
    attend(far_seq, 1, 1)
    send("ctx", "ctx", ctx_out.at[1, core], ctx_in.at[FAR], across)
    send("ctx", "ctx", ctx_out.at[1, 1 - core], ctx_in.at[FARSIB], diagonal)
    relay(0)
    loaded("own", x.at[pl.ds(2 * seq, 2)])
    project(seq, 0, OWN, True)
    relay(1)
    send_part(6, 7)
    attend(seq, 0, 0)
    send("ctx", "ctx", ctx_out.at[0, 1 - core], ctx_in.at[SIB], sibling)
    ctx_in[OWN] = ctx_out[0, core]
    relay(2)
    send_part(8)
    send_rest(1, 2)
    relay(3)
    send_rest(3, 4)
    collect(0)
    relay(4)
    relay(5)
    send_rest(5, 6)

    loaded("w", w.at[OWN, pl.ds(0, QKV)])
    loaded("one", gains.at[0])
    loaded("two", gains.at[1])
    loaded("cot", cot)
    arrived("so", w.at[SIB, pl.ds(OUT, 1)])
    collect_sibling(0)
    arrived("ctx", ctx_in.at[pl.ds(1, 3)])
    attn = dot(ctx_in[...].reshape(768, 256), w[:, OUT].reshape(768, 768), 0, 0)
    n1, r1 = norm(x[h].astype(F32) + attn)
    normed_one[...] = n1
    inverse_one[...] = r1
    h1 = n1 * gains[0:1]
    hidden[...] = h1
    hidden_low[...] = h1.astype(BF16)

    def go_up(slot):
        up = dot(hidden_low[...], w[slot, UP : UP + 4].reshape(768, 768))
        phi = 0.5 * (1.0 + lax.erf(up * 0.7071067811865476))
        slope[slot] = phi + up * (0.3989422804014327 * jnp.exp(-0.5 * up * up))
        act[slot] = (up * phi).astype(BF16)

    def go_down(slot):
        return dot(act[slot], w[slot, DOWN : DOWN + 4].reshape(768, 768))

    relay(6)
    send_part(9)
    send_rest(7, 8)
    go_up(OWN)
    relay(7)
    send_part(10)
    arrived("su", w.at[SIB, pl.ds(UP, 4)])
    go_up(SIB)
    relay(8)
    send_part(11)
    send_rest(9, 10, 11)
    arrived("sd", w.at[SIB, pl.ds(DOWN, 4)])
    total[...] = hidden[...] + go_down(OWN) + go_down(SIB)
    collect(1)
    go_up(FAR)
    collect_sibling(1)
    go_up(FARSIB)
    collect(2)
    relay(9)
    collect(3)
    total[...] += go_down(FAR)
    collect_sibling(2)
    collect_sibling(3)
    z2 = total[...] + go_down(FARSIB)

    n2, r2 = norm(z2)
    position = lax.broadcasted_iota(jnp.int32, (256, 1), 0) + 256 * core
    valid = (position < lengths[seq]).astype(F32)
    activations[h] = (valid * (n2 * gains[1:2])).astype(BF16)
    send("rows", "ay", activations.at[h], activations.at[h], across)
    send("rows", "all", activations.at[h], activations.at[h], sibling)
    d_z2 = norm_back(cot[...].astype(F32) * valid * gains[1:2], n2, r2)
    d_z2_low = d_z2.astype(BF16)
    relay(10)

    steps = []
    for slot in range(4):
        d_act = dot(d_z2_low, w[slot, DOWN : DOWN + 4].reshape(768, 768), 1, 1)
        steps.append((d_act * slope[slot]).astype(BF16))
    grad_h1 = d_z2
    for slot in range(4):
        grad_h1 = grad_h1 + dot(steps[slot], w[slot, UP : UP + 4].reshape(768, 768), 1, 1)

    d_z1 = norm_back(grad_h1 * gains[0:1], normed_one[...], inverse_one[...])
    grad_z1[...] = d_z1
    d_ctx = dot(w[:, OUT].reshape(768, 768), d_z1.astype(BF16), 1, 1).astype(BF16)
    dctx_out[...] = d_ctx.reshape(4, 192, 256)
    send("dctx", "dctx", dctx_out.at[SIB], dctx_in.at[core, 0], sibling)
    send("dctx", "dctx", dctx_out.at[FARSIB], dctx_in.at[core, 1], sibling)
    dctx_in[core, 0] = dctx_out[OWN]
    dctx_in[core, 1] = dctx_out[FAR]
    relay(11)
    arrived("dctx", dctx_in.at[1 - core])

    def attend_back(which):
        d_scores = []
        for head in range(3):
            rows = head_rows(0, head)
            d_out = jnp.concatenate([dctx_in[0, which, rows], dctx_in[1, which, rows]], axis=1)
            probability = probs[which, head].astype(F32)
            d_weights = dot(qkv[which, head_rows(2, head)], d_out, 0, 0)
            mean = jnp.sum(probability * d_weights, axis=0, keepdims=True)
            d_scores.append((probability * (d_weights - mean)).astype(BF16))
        for head in range(3):
            rows = head_rows(0, head)
            d_out = jnp.concatenate([dctx_in[0, which, rows], dctx_in[1, which, rows]], axis=1)
            d_query = (0.125 * dot(qkv[which, head_rows(1, head)], d_scores[head])).astype(BF16)
            d_key = 0.125 * dot(d_scores[head], qkv[which, head_rows(0, head)], 1, 1)
            d_value = dot(probs[which, head], d_out, 1, 1)
            pieces = (d_query, d_key.astype(BF16).T, d_value.astype(BF16).T)
            for j, piece in enumerate(pieces):
                for half in range(2):
                    span = slice(256 * half, 256 * half + 256)
                    grad_qkv[which, half, head_rows(j, head)] = piece[:, span]

    def adapter_grads(which):
        for j in range(2):
            rows = slice(384 * j, 384 * j + 192)
            grads[which, j] = 2.0 * (
                dot(low[:, :256], grad_qkv[which, 0, rows], 1, 1)
                + dot(low[:, 256:], grad_qkv[which, 1, rows], 1, 1)
            )

    def batch_start(s):
        send("g", ("g", s), grads.at[0 if s == 0 else 1 + s], grads_in.at[1 + s], batch_peers[s])

    def batch_end(s):
        arrived(("g", s), grads_in.at[1 + s])
        grads[2 + s] = grads[0 if s == 0 else 1 + s] + grads_in[1 + s]

    attend_back(0)
    adapter_grads(0)

    collect(4)
    arrived("b", adapter_up.at[1])
    project(seq, 1, FAR, False)
    attend(seq, 1, None)
    arrived("ay", activations.at[flip(h, 2)])
    send("rows", "all", activations.at[flip(h, 2)], activations.at[flip(h, 2)], sibling)
    attend_back(1)
    adapter_grads(1)
    send("g", "g", grads.at[1], grads_in.at[0], across)

    def adapter_rows(half):
        d_low = 0.0
        for which in range(2):
            d_low = d_low + dot(adapter_up[which].astype(BF16), grad_qkv[which, half, :576])
        d_low = 2.0 * d_low
        coarse = d_low.astype(BF16)
        fine = (d_low - coarse.astype(F32)).astype(BF16)
        grad_qkv[0, half, 576:] = jnp.concatenate([coarse, fine], axis=0)

    def input_part(half, t):
        span = slice(128 * t, 128 * t + 128)
        return dot(grad_qkv[0, half][:, span], adapted(OWN, 608), 0, 0) + dot(
            grad_qkv[1, half, :576][:, span], adapted(FAR, 576), 0, 0
        )

    adapter_rows(1 - core)
    for t in range(2):
        part_out[t] = input_part(1 - core, t).astype(BF16)
        send("rows", ("p", t), part_out.at[t], part_in.at[t], sibling)
    adapter_rows(core)
    for t in range(2):
        span = slice(128 * t, 128 * t + 128)
        own = grad_z1[span] + input_part(core, t)
        arrived(("p", t), part_in.at[t])
        input_grad[h, span] = (own + part_in[t].astype(F32)).astype(BF16)
        for n, (first, count) in enumerate(CHUNKS):
            if first // 128 == t:
                block = input_grad.at[h, pl.ds(first, count)]
                send("rows", ("i", n), block, block, across)
    send("rows", "all", input_grad.at[h], input_grad.at[h], sibling)

    def pass_on(n):
        first, count = CHUNKS[n]
        block = input_grad.at[flip(h, 2), pl.ds(first, count)]
        arrived(("i", n), block)
        send("rows", "all", block, block, sibling)

    arrived("g", grads_in.at[0])
    grads[0] += grads_in[0]
    batch_start(0)
    for s in range(batch_steps):
        batch_end(s)
        if s + 1 < batch_steps:
            batch_start(s + 1)
        if s == 1:
            pass_on(0)
    final = grads[1 + batch_steps]
    grads_out[0] = final[0, 0:8]
    grads_out[1] = final[1, 8:16]
    for n in range(1, len(CHUNKS)):
        pass_on(n)
    arrived("all", activations)

    sent("y", w.at[FAR, pl.ds(0, 3)])
    sent("x", w.at[FAR, pl.ds(0, 3)])
    sent("z", w.at[FAR, pl.ds(0, 3)])
    sent("t", w.at[FAR, pl.ds(0, 3), pl.ds(0, 96)])
    sent("d", w.at[FAR, pl.ds(0, 3), pl.ds(0, 96)])
    sent("c", w.at[FAR, pl.ds(0, 9)])
    sent("w", w.at[SIB, pl.ds(0, 9)])
    sent("ctx", ctx_in.at[pl.ds(0, 3)])
    sent("dctx", dctx_in.at[0])
    sent("rows", w.at[pl.ds(0, 4), pl.ds(0, 7), pl.ds(0, 64)])
    sent("b", adapter_up.at[0])
    sent("g", grads_in)


def hand_over(activations, input_grad, grads, *rest):
    targets, sem = rest[:4], rest[4]
    sources = (activations, input_grad, grads.at[0], grads.at[1])
    copies = [
        pltpu.make_async_copy(source, target, sem.at[n])
        for n, (source, target) in enumerate(zip(sources, targets))
    ]
    for c in copies:
        c.start()
    for c in copies:
        c.wait()


def body(batch_steps, *given):
    (
        tokens,
        lengths,
        w_query,
        w_key,
        w_value,
        w_out,
        down_query,
        down_value,
        up_query,
        up_value,
        w_up,
        w_down,
        gain_attn,
        gain_ffn,
        cotangent,
    ) = given
    anywhere = pl.BlockSpec(memory_space=pl.ANY)
    in_vmem = pl.BlockSpec(memory_space=pltpu.VMEM)
    in_hbm = pl.BlockSpec(memory_space=pltpu.HBM)
    vmem = pltpu.VMEM
    results = pl.pallas_call(
        functools.partial(kernel, batch_steps),
        out_shape=(
            vmem((4, 256, 768), BF16),
            vmem((4, 256, 768), BF16),
            vmem((2, 8, 192), F32),
        ),
        in_specs=[pl.BlockSpec(memory_space=pltpu.SMEM)] + [in_hbm] * 14,
        out_specs=(in_vmem,) * 3,
        scratch_shapes=[
            vmem((4, 256, 768), BF16),
            vmem((4, 13, 192, 768), BF16),
            vmem((2, 8, 768), BF16),
            vmem((2, 8, 192), BF16),
            vmem((2, 768), F32),
            vmem((256, 768), BF16),
            vmem((2, 16, 576), F32),
            vmem((16, 512), BF16),
            vmem((2, 576, 512), BF16),
            vmem((2, 3, 512, 512), BF16),
            vmem((2, 2, 192, 256), BF16),
            vmem((4, 192, 256), BF16),
            vmem((256, 768), F32),
            vmem((256, 1), F32),
            vmem((256, 768), F32),
            vmem((256, 768), BF16),
            vmem((4, 256, 768), BF16),
            vmem((4, 256, 768), F32),
            vmem((256, 768), F32),
            vmem((256, 768), F32),
            vmem((4, 192, 256), BF16),
            vmem((2, 2, 192, 256), BF16),
            vmem((2, 2, 608, 256), BF16),
            vmem((2, 128, 768), BF16),
            vmem((2, 128, 768), BF16),
            vmem((2 + batch_steps, 2, 16, 192), F32),
            vmem((1 + batch_steps, 2, 16, 192), F32),
            pltpu.SemaphoreType.DMA((9,)),
            pltpu.SemaphoreType.DMA((len(SEND_GROUPS),)),
            pltpu.SemaphoreType.DMA((35 + batch_steps,)),
        ],
        compiler_params=pltpu.CompilerParams(
            collective_id=0, has_side_effects=True, vmem_limit_bytes=56 * 1024 * 1024
        ),
        cost_estimate=pl.CostEstimate(
            flops=11_000_000_000, bytes_accessed=20_000_000, transcendentals=4_000_000
        ),
    )(
        lengths,
        tokens.reshape(4, 256, 768),
        w_query.T,
        w_key.T,
        w_value.T,
        w_out.reshape(1, 192, 768),
        w_up.reshape(4, 192, 768),
        w_down.reshape(4, 192, 768),
        down_query.T,
        down_value.T,
        up_query,
        up_value,
        gain_attn,
        gain_ffn,
        cotangent.reshape(4, 256, 768),
    )
    rows = jax.ShapeDtypeStruct((4, 256, 768), BF16)
    small = jax.ShapeDtypeStruct((8, 192), F32)
    activations, input_grad, grad_b_query, grad_b_value = pl.pallas_call(
        hand_over,
        out_shape=(rows, rows, small, small),
        in_specs=[anywhere] * 3,
        out_specs=[in_hbm] * 4,
        scratch_shapes=[pltpu.SemaphoreType.DMA((4,))],
        compiler_params=pltpu.CompilerParams(vmem_limit_bytes=1024 * 1024),
    )(*results)
    return (
        activations.reshape(tokens.shape),
        input_grad.reshape(tokens.shape),
        grad_b_query,
        grad_b_value,
    )


def solution(mesh):
    batch_steps = mesh.shape["batch"].bit_length() - 1
    in_specs = (
        P("batch", None),
        P("batch"),
        P(None, "head"),
        P(None, "head"),
        P(None, "head"),
        P("head", None),
        P(),
        P(),
        P(None, "head"),
        P(None, "head"),
        P(None, "head"),
        P("head", None),
        P(),
        P(),
        P("batch", None),
    )
    out_specs = (P("batch", None), P("batch", None), P(None, "head"), P(None, "head"))
    return jax.shard_map(
        functools.partial(body, batch_steps),
        mesh=mesh,
        in_specs=in_specs,
        out_specs=out_specs,
        check_vma=False,
    )
```

```python
import functools

import jax
import jax.numpy as jnp
from jax import lax
from jax.experimental import pallas as pl
from jax.experimental.pallas import tpu as pltpu
from jax.sharding import PartitionSpec as P

HD = 64
BF16 = jnp.bfloat16
F32 = jnp.float32
MESH = pl.DeviceIdType.MESH

OUT, UP, DOWN, QKV, ADAPTER = 0, 1, 5, 9, 12
ITEMS = 12
OWN, SIB, FAR, FARSIB = 0, 1, 2, 3
OVER_Y = (16, 0, 0, 0, 0, 32, 32, 32, 32, 32, 32, 32)
TWICE = (1, 2, 3, 4)
GROUPS = ((0, 1), (1, 2), (3, 2), (5, 2), (7, 1), (8, 1), (9, 3))
SPANS = ((0, 128), (128, 256), (384, 384))
PIECES = ((0, 128), (128, 256), (384, 256), (640, 128))
SEND_GROUPS = ("y", "x", "z", "t", "d", "c", "w", "ctx", "dctx", "rows", "b", "l", "g")


def dot(left, right, left_dim=1, right_dim=0):
    return lax.dot_general(
        left, right, (((left_dim,), (right_dim,)), ((), ())), preferred_element_type=F32
    )


def norm(z):
    centre = z - jnp.mean(z, axis=-1, keepdims=True)
    inverse = lax.rsqrt(jnp.mean(centre * centre, axis=-1, keepdims=True) + 1e-05)
    return centre * inverse, inverse


def norm_back(scaled, normed, inverse):
    return inverse * (
        scaled
        - jnp.mean(scaled, axis=-1, keepdims=True)
        - normed * jnp.mean(scaled * normed, axis=-1, keepdims=True)
    )


def flip(index, bit):
    return index + bit - 2 * bit * ((index // bit) % 2)


def kernel(
    batch,
    lengths,
    tokens,
    w_query,
    w_key,
    w_value,
    w_out,
    w_up,
    w_down,
    down_query,
    down_value,
    up_query,
    up_value,
    gain_one,
    gain_two,
    cotangent,
    activations,
    input_grad,
    grads_out,
    x,
    w,
    raw_down,
    raw_up,
    gains,
    cot,
    adapter_up,
    low,
    qkv,
    probs,
    log_sum,
    ctx_out,
    ctx_in,
    normed_one,
    inverse_one,
    hidden,
    hidden_low,
    act,
    slope,
    total,
    grad_z1,
    input_sum,
    dctx_out,
    dctx_in,
    grad_qkv,
    part_out,
    part_in,
    grads,
    grads_in,
    grads_all,
    grads_sums,
    local_sem,
    send_sem,
    recv_sem,
):
    b = lax.axis_index("batch")
    h = lax.axis_index("head")
    core = h % 2
    seq = h // 2
    far_seq = 1 - seq
    part = b % 4
    sibling = (b, flip(h, 1))
    across = (b, flip(h, 2))
    diagonal = (b, 3 - h)
    x_peer = (flip(b, 1), h)
    z_peer = (flip(b, 2), h)
    xz_peer = (flip(flip(b, 1), 2), h)
    batch_peers = [(flip(b, 1 << s), h) for s in range(2, batch.bit_length() - 1)]

    barrier = pltpu.get_barrier_semaphore()
    peers = [sibling, across, diagonal, x_peer, z_peer, xz_peer] + batch_peers
    for peer in peers:
        pl.semaphore_signal(barrier, inc=1, device_id=peer, device_id_type=MESH)

    recv_numbers = {}
    local_numbers = {}

    def copy(group, key, source, target, device):
        number = recv_numbers.setdefault(key, len(recv_numbers))
        return pltpu.make_async_remote_copy(
            src_ref=source,
            dst_ref=target,
            send_sem=send_sem.at[SEND_GROUPS.index(group)],
            recv_sem=recv_sem.at[number],
            device_id=device,
            device_id_type=MESH,
        )

    def send(group, key, source, target, device):
        copy(group, key, source, target, device).start()

    def arrived(key, target):
        copy("y", key, target, target, sibling).wait_recv()

    def sent(group, ref):
        copy(group, ("y", 0), ref, ref, sibling).wait_send()

    def local(key, source, target):
        number = local_numbers.setdefault(key, len(local_numbers))
        return pltpu.make_async_copy(source, target, local_sem.at[number])

    def load(key, source, target):
        local(key, source, target).start()

    def loaded(key, target):
        local(key, target, target).wait()

    for j, ref in enumerate((w_query, w_key, w_value)):
        load("qkv", ref, w.at[OWN, QKV + j])
    load("far", tokens.at[pl.ds(2 * far_seq, 2)], x.at[pl.ds(2 * far_seq, 2)])
    load("downs", down_query, raw_down.at[0])
    load("downs", down_value, raw_down.at[1])
    load("ups", up_query, raw_up.at[0])
    load("ups", up_value, raw_up.at[1])
    load("own", tokens.at[pl.ds(2 * seq, 2)], x.at[pl.ds(2 * seq, 2)])
    load("w", w_out, w.at[OWN, pl.ds(OUT, 1)])
    load("w", w_up, w.at[OWN, pl.ds(UP, 4)])
    load("w", w_down, w.at[OWN, pl.ds(DOWN, 4)])
    load("one", gain_one, gains.at[0])
    load("two", gain_two, gains.at[1])
    load("cot", cotangent.at[h], cot)

    far = w.at[FAR]
    px, pz, pd = flip(part, 1), flip(part, 2), 3 - part
    group_of = {}
    for first, count in GROUPS:
        for item in range(first, first + count):
            group_of[item] = first

    def rows_of(ref, item, index, start=0, count=48):
        return ref.at[item, pl.ds(pl.multiple_of(48 * index + start, 16), count)]

    def source_of(item):
        if item >= QKV:
            return w.at[OWN], item
        if item >= DOWN:
            return w_down, item - DOWN
        if item >= UP:
            return w_up, item - UP
        return w_out, item

    def send_part(*items):
        for item in items:
            source, at = source_of(item)
            mine, theirs = rows_of(source, at, part), rows_of(far, item, part)
            send("y", ("y", item), mine, theirs, across)

    def send_rest(*items):
        for item in items:
            source, at = source_of(item)
            count = OVER_Y[item]
            mine, theirs = rows_of(source, at, pd, 0, count), rows_of(far, item, pd, 0, count)
            send("t", ("f", group_of[item]), mine, theirs, across)

    def relay(*items):
        for item in items:
            mine = rows_of(far, item, part)
            arrived(("y", item), mine)
            twice = item in TWICE
            key = ("f", group_of[item])
            send("x", ("x", item) if twice else key, mine, mine, x_peer)
            send("z", ("z", item) if twice else key, mine, mine, z_peer)
            if not twice:
                count = OVER_Y[item]
                rest = rows_of(far, item, part, count, 48 - count)
                send("d", key, rest, rest, xz_peer)

    def relay_again(*items):
        for item in items:
            key = ("f", group_of[item])
            arrived(("x", item), rows_of(far, item, px))
            over_x = 32 if item % 2 else 16
            piece = rows_of(far, item, px, over_x, 48 - over_x)
            send("z", key, piece, piece, z_peer)
            arrived(("z", item), rows_of(far, item, pz))
            piece = rows_of(far, item, pz, 0, over_x)
            send("x", key, piece, piece, x_peer)

    def collect(group):
        first, count = GROUPS[group]
        items = pl.ds(first, count)
        arrived(("f", first), w.at[FAR, items, pl.ds(0, 48 if first in TWICE else 144)])
        if first < QKV:
            send("c", ("c", first), w.at[FAR, items], w.at[FARSIB, items], sibling)

    def collect_sibling(group):
        first, count = GROUPS[group]
        arrived(("c", first), w.at[FARSIB, pl.ds(first, count)])

    pl.semaphore_wait(barrier, len(peers))
    send_part(0)
    send_part(1)
    send_rest(0)
    send_part(2)
    send_part(3)
    send_part(4)
    send_part(5)
    send_part(6)
    send_part(7)
    send("w", "so", w_out, w.at[SIB, pl.ds(OUT, 1)], sibling)
    send("w", "su", w_up, w.at[SIB, pl.ds(UP, 4)], sibling)
    send("w", "sd", w_down, w.at[SIB, pl.ds(DOWN, 4)], sibling)

    loaded("downs", raw_down)
    loaded("ups", raw_up)
    downs = jnp.concatenate([raw_down[0].astype(F32), raw_down[1].astype(F32)] * 2, axis=0)
    w[OWN, ADAPTER, :32] = downs.astype(BF16)
    w[FAR, ADAPTER, :32] = downs.astype(BF16)
    nothing = jnp.zeros((8, 192), F32)
    adapter_up[0, :, :192] = jnp.concatenate([raw_up[0].astype(F32), nothing], axis=0)
    adapter_up[0, :, 192:384] = jnp.zeros((16, 192), F32)
    adapter_up[0, :, 384:] = jnp.concatenate([nothing, raw_up[1].astype(F32)], axis=0)

    def adapted(slot, count):
        return w[slot, QKV:].reshape(768, 768)[:count]

    def project(rows, which, slot, store):
        full = dot(adapted(slot, 592), x[pl.ds(2 * rows, 2)].reshape(512, 768), 1, 1)
        lows = full[576:].astype(BF16)
        ups = adapter_up[0 if slot == OWN else 1].astype(BF16)
        if store:
            low[...] = lows
        query = full[:192] + 2.0 * dot(ups[:, :192], lows, 0, 0)
        value = full[384:576] + 2.0 * dot(ups[:, 384:], lows, 0, 0)
        qkv[which, :192] = query.astype(BF16)
        qkv[which, 192:384] = full[192:384].astype(BF16)
        qkv[which, 384:] = value.astype(BF16)

    def head_rows(j, head):
        return slice(192 * j + HD * head, 192 * j + HD * (head + 1))

    def scores_of(rows, which, head):
        position = lax.broadcasted_iota(jnp.int32, (512, 1), 0)
        bias = jnp.where(position < lengths[rows], 0.0, -1e30)
        query = qkv[which, head_rows(0, head)] * jnp.asarray(0.125, BF16)
        return dot(qkv[which, head_rows(1, head)], query, 0, 0) + bias

    def attend(rows, which, context):
        for head in range(3):
            scores = scores_of(rows, which, head)
            top = jnp.max(scores, axis=0, keepdims=True)
            exponent = jnp.exp(scores - top)
            amount = jnp.sum(exponent, axis=0, keepdims=True)
            probs[which, head] = (exponent * (1.0 / amount)).astype(BF16)
            if which == 1:
                log_sum[0, head] = top + jnp.log(amount)
        for head in range(3):
            out = dot(qkv[which, head_rows(2, head)], probs[which, head]).astype(BF16)
            ctx_out[context, 0, head_rows(0, head)] = out[:, :256]
            ctx_out[context, 1, head_rows(0, head)] = out[:, 256:]

    loaded("qkv", w.at[OWN, pl.ds(QKV, 3)])
    loaded("far", x.at[pl.ds(2 * far_seq, 2)])
    project(far_seq, 1, OWN, False)
    attend(far_seq, 1, 1)
    send("ctx", "ctx", ctx_out.at[1, core], ctx_in.at[FAR], across)
    send("ctx", "ctx", ctx_out.at[1, 1 - core], ctx_in.at[FARSIB], diagonal)
    send_part(8)
    send_rest(5)
    send_rest(6)
    send_rest(7)
    send_rest(8)
    send_part(9)
    send_part(10)
    send_part(11)
    send_rest(9)
    send_rest(10)
    send_rest(11)
    send("b", "b", adapter_up.at[0], adapter_up.at[1], across)
    send("l", "l", log_sum.at[0], log_sum.at[1], across)
    relay(0)
    loaded("own", x.at[pl.ds(2 * seq, 2)])
    project(seq, 0, OWN, True)
    relay(1)
    attend(seq, 0, 0)
    send("ctx", "ctx", ctx_out.at[0, 1 - core], ctx_in.at[SIB], sibling)
    ctx_in[OWN] = ctx_out[0, core]
    relay(2)
    relay(3)
    relay_again(1)
    relay(4)
    relay_again(2)
    relay(5)
    collect(0)
    relay_again(3)
    relay(6)
    relay_again(4)
    relay(7)

    loaded("w", w.at[OWN, pl.ds(0, QKV)])
    loaded("one", gains.at[0])
    loaded("two", gains.at[1])
    loaded("cot", cot)
    arrived("so", w.at[SIB, pl.ds(OUT, 1)])
    collect_sibling(0)
    arrived("ctx", ctx_in.at[pl.ds(1, 3)])
    attn = dot(ctx_in[...].reshape(768, 256), w[:, OUT].reshape(768, 768), 0, 0)
    n1, r1 = norm(x[h].astype(F32) + attn)
    normed_one[...] = n1
    inverse_one[...] = r1
    h1 = n1 * gains[0:1]
    hidden[...] = h1
    hidden_low[...] = h1.astype(BF16)

    def go_up(slot):
        up = dot(hidden_low[...], w[slot, UP : UP + 4].reshape(768, 768))
        phi = 0.5 * (1.0 + lax.erf(up * 0.7071067811865476))
        slope[slot] = phi + up * (0.3989422804014327 * jnp.exp(-0.5 * up * up))
        act[slot] = (up * phi).astype(BF16)

    def go_down(slot, first=0, count=4):
        rows = slice(192 * first, 192 * (first + count))
        weights = w[slot, DOWN + first : DOWN + first + count].reshape(192 * count, 768)
        return dot(act[slot, :, rows], weights)

    go_up(OWN)
    arrived("su", w.at[SIB, pl.ds(UP, 4)])
    go_up(SIB)
    arrived("sd", w.at[SIB, pl.ds(DOWN, 4)])
    total[...] = hidden[...] + go_down(OWN) + go_down(SIB)
    relay(8)
    collect(1)
    collect(2)
    go_up(FAR)
    collect_sibling(1)
    collect_sibling(2)
    go_up(FARSIB)
    collect(3)
    collect(4)
    collect(5)
    total[...] += go_down(FAR, 0, 3)
    collect_sibling(3)
    collect_sibling(4)
    total[...] += go_down(FARSIB, 0, 3)
    total[...] += go_down(FAR, 3, 1)
    relay(9)
    collect_sibling(5)
    z2 = total[...] + go_down(FARSIB, 3, 1)

    n2, r2 = norm(z2)
    position = lax.broadcasted_iota(jnp.int32, (256, 1), 0) + 256 * core
    valid = (position < lengths[seq]).astype(F32)
    activations[h] = (valid * (n2 * gains[1:2])).astype(BF16)
    send("rows", "ay", activations.at[h], activations.at[h], across)
    send("rows", "all", activations.at[h], activations.at[h], sibling)
    d_z2 = norm_back(cot[...].astype(F32) * valid * gains[1:2], n2, r2)
    d_z2_low = d_z2.astype(BF16)
    relay(10)

    steps = []
    for slot in range(4):
        d_act = dot(d_z2_low, w[slot, DOWN : DOWN + 4].reshape(768, 768), 1, 1)
        steps.append((d_act * slope[slot]).astype(BF16))
    grad_h1 = d_z2
    for slot in range(4):
        grad_h1 = grad_h1 + dot(steps[slot], w[slot, UP : UP + 4].reshape(768, 768), 1, 1)

    d_z1 = norm_back(grad_h1 * gains[0:1], normed_one[...], inverse_one[...])
    grad_z1[...] = d_z1
    d_z1_low = d_z1.astype(BF16)
    relay(11)

    def d_context(first):
        pair = [w[first, OUT], w[first + 2, OUT]]
        d_ctx = dot(jnp.concatenate(pair, axis=0), d_z1_low, 1, 1).astype(BF16)
        dctx_out[first] = d_ctx[:192]
        dctx_out[first + 2] = d_ctx[192:]

    d_context(SIB)
    send("dctx", "dctx", dctx_out.at[SIB], dctx_in.at[core, 0], sibling)
    send("dctx", "dctx", dctx_out.at[FARSIB], dctx_in.at[core, 1], sibling)
    d_context(OWN)
    dctx_in[core, 0] = dctx_out[OWN]
    dctx_in[core, 1] = dctx_out[FAR]
    arrived("dctx", dctx_in.at[1 - core])

    def attend_back(which):
        d_scores = []
        for head in range(3):
            rows = head_rows(0, head)
            d_out = jnp.concatenate([dctx_in[0, which, rows], dctx_in[1, which, rows]], axis=1)
            if which == 0:
                probability = probs[0, head].astype(F32)
            else:
                probability = jnp.exp(scores_of(seq, 1, head) - log_sum[1, head])
                probs[1, head] = probability.astype(BF16)
            d_weights = dot(qkv[which, head_rows(2, head)], d_out, 0, 0)
            mean = jnp.sum(probability * d_weights, axis=0, keepdims=True)
            d_scores.append((probability * (d_weights - mean)).astype(BF16))
        for head in range(3):
            rows = head_rows(0, head)
            d_out = jnp.concatenate([dctx_in[0, which, rows], dctx_in[1, which, rows]], axis=1)
            d_query = (0.125 * dot(qkv[which, head_rows(1, head)], d_scores[head])).astype(BF16)
            d_key = 0.125 * dot(d_scores[head], qkv[which, head_rows(0, head)], 1, 1)
            d_value = dot(probs[which, head], d_out, 1, 1)
            pieces = (d_query, d_key.astype(BF16).T, d_value.astype(BF16).T)
            for j, piece in enumerate(pieces):
                grad_qkv[which, head_rows(j, head)] = piece

    def adapter_grads(which):
        for j in range(2):
            rows = slice(384 * j, 384 * j + 192)
            both = dot(low[...], grad_qkv[which, rows], 1, 1)
            grads[which, j] = 2.0 * both[8 * j : 8 * j + 8]

    def adapter_rows(which):
        d_low = 2.0 * dot(adapter_up[which].astype(BF16), grad_qkv[which, :576])
        coarse = d_low.astype(BF16)
        fine = (d_low - coarse.astype(F32)).astype(BF16)
        grad_qkv[which, 576:] = jnp.concatenate([coarse, fine], axis=0)

    def input_part(which, columns, half=None):
        weights = w[OWN if which == 0 else FAR, QKV:].reshape(768, 768)[:608, columns]
        if half is None:
            return dot(grad_qkv[which], weights, 0, 0).reshape(2, 256, 768)
        rows = pl.ds(pl.multiple_of(256 * half, 256), 256)
        return dot(grad_qkv[which, :, rows], weights, 0, 0)

    attend_back(0)
    adapter_rows(0)
    input_sum[...] = input_part(0, slice(0, 768))
    input_sum[core] += grad_z1[...]
    adapter_grads(0)

    collect(6)
    arrived("b", adapter_up.at[1])
    arrived("l", log_sum.at[1])
    project(seq, 1, FAR, False)
    attend_back(1)
    adapter_rows(1)
    spans = [(t, slice(first, first + count)) for t, (first, count) in enumerate(SPANS)]
    pieces = [(n, slice(first, first + count)) for n, (first, count) in enumerate(PIECES)]
    for t, columns in spans:
        given = input_sum[1 - core, :, columns] + input_part(1, columns, 1 - core)
        part_out[:, columns] = given.astype(BF16)
        send("rows", ("p", t), part_out.at[:, columns], part_in.at[:, columns], sibling)
        if t == 0:
            adapter_grads(1)
            send("g", "g", grads.at[1], grads_in, across)
    for t, columns in spans:
        own = input_sum[core, :, columns] + input_part(1, columns, core)
        arrived(("p", t), part_in.at[:, columns])
        input_grad[h, :, columns] = (own + part_in[:, columns].astype(F32)).astype(BF16)
        for n, piece in pieces:
            if columns.start <= piece.start < columns.stop:
                block = input_grad.at[h, :, piece]
                send("rows", ("i", n), block, block, across)
    send("rows", "all", input_grad.at[h], input_grad.at[h], sibling)

    def pass_on(n):
        block = input_grad.at[flip(h, 2), :, pieces[n][1]]
        arrived(("i", n), block)
        send("rows", "all", block, block, sibling)

    arrived("ay", activations.at[flip(h, 2)])
    send("rows", "all", activations.at[flip(h, 2)], activations.at[flip(h, 2)], sibling)
    arrived("g", grads_in)
    grads_all[part] = grads[0] + grads_in[...]
    for peer in (x_peer, z_peer, xz_peer):
        send("g", "sums", grads_all.at[part], grads_all.at[part], peer)
    pass_on(0)
    arrived("sums", grads_all.at[pl.ds(0, 3)])
    sums = (grads_all[0] + grads_all[1]) + (grads_all[2] + grads_all[3])
    for n, peer in enumerate(batch_peers):
        grads_sums[2 * n] = sums
        send("g", ("g", n), grads_sums.at[2 * n], grads_sums.at[2 * n + 1], peer)
        if n == 0:
            for m in range(1, len(pieces)):
                pass_on(m)
        arrived(("g", n), grads_sums.at[2 * n + 1])
        sums = sums + grads_sums[2 * n + 1]
    grads_out[...] = sums
    for n in range(1, 1 if batch_peers else len(pieces)):
        pass_on(n)
    arrived("all", activations)

    def rows_block(count):
        tiles = count // 16
        shapes = [(m, n, tiles // (m * n)) for m in (1, 2, 3, 4) for n in range(1, 13) if tiles % (m * n) == 0]
        inner, outer, depth = next(shape for shape in shapes if shape[2] <= 12)
        return w.at[pl.ds(0, inner), pl.ds(0, outer), pl.ds(0, 16 * depth)]

    sent("y", w.at[FAR, pl.ds(0, 3)])
    sent("x", rows_block(48 * ITEMS + 24 * len(TWICE)))
    sent("z", rows_block(48 * ITEMS + 24 * len(TWICE)))
    sent("t", rows_block(sum(OVER_Y)))
    sent("d", rows_block(sum(48 - OVER_Y[n] for n in range(ITEMS) if n not in TWICE)))
    sent("c", w.at[FAR, pl.ds(0, 9)])
    sent("w", w.at[SIB, pl.ds(0, 9)])
    sent("ctx", ctx_in.at[pl.ds(0, 3)])
    sent("dctx", dctx_in.at[0])
    sent("rows", w.at[pl.ds(0, 4), pl.ds(0, 7), pl.ds(0, 64)])
    sent("b", adapter_up.at[0])
    sent("l", log_sum.at[0])
    sent("g", grads_sums.at[pl.ds(0, 4 + len(batch_peers))])


def hand_over(activations, input_grad, grads, *rest):
    targets, sem = rest[:4], rest[4]
    sources = (activations, input_grad, grads.at[0], grads.at[1])
    copies = [
        pltpu.make_async_copy(source, target, sem.at[n])
        for n, (source, target) in enumerate(zip(sources, targets))
    ]
    for c in copies:
        c.start()
    for c in copies:
        c.wait()


def body(batch, *given):
    (
        tokens,
        lengths,
        w_query,
        w_key,
        w_value,
        w_out,
        down_query,
        down_value,
        up_query,
        up_value,
        w_up,
        w_down,
        gain_attn,
        gain_ffn,
        cotangent,
    ) = given
    anywhere = pl.BlockSpec(memory_space=pl.ANY)
    in_vmem = pl.BlockSpec(memory_space=pltpu.VMEM)
    in_hbm = pl.BlockSpec(memory_space=pltpu.HBM)
    vmem = pltpu.VMEM
    results = pl.pallas_call(
        functools.partial(kernel, batch),
        out_shape=(
            vmem((4, 256, 768), BF16),
            vmem((4, 256, 768), BF16),
            vmem((2, 8, 192), F32),
        ),
        in_specs=[pl.BlockSpec(memory_space=pltpu.SMEM)] + [in_hbm] * 14,
        out_specs=(in_vmem,) * 3,
        scratch_shapes=[
            vmem((4, 256, 768), BF16),
            vmem((4, 13, 192, 768), BF16),
            vmem((2, 8, 768), BF16),
            vmem((2, 8, 192), BF16),
            vmem((2, 768), F32),
            vmem((256, 768), BF16),
            vmem((2, 16, 576), F32),
            vmem((16, 512), BF16),
            vmem((2, 576, 512), BF16),
            vmem((2, 3, 512, 512), BF16),
            vmem((2, 3, 1, 512), F32),
            vmem((2, 2, 192, 256), BF16),
            vmem((4, 192, 256), BF16),
            vmem((256, 768), F32),
            vmem((256, 1), F32),
            vmem((256, 768), F32),
            vmem((256, 768), BF16),
            vmem((4, 256, 768), BF16),
            vmem((4, 256, 768), F32),
            vmem((256, 768), F32),
            vmem((256, 768), F32),
            vmem((2, 256, 768), F32),
            vmem((4, 192, 256), BF16),
            vmem((2, 2, 192, 256), BF16),
            vmem((2, 608, 512), BF16),
            vmem((256, 768), BF16),
            vmem((256, 768), BF16),
            vmem((2, 2, 8, 192), F32),
            vmem((2, 8, 192), F32),
            vmem((4, 2, 8, 192), F32),
            vmem((2 * batch.bit_length(), 2, 8, 192), F32),
            pltpu.SemaphoreType.DMA((9,)),
            pltpu.SemaphoreType.DMA((len(SEND_GROUPS),)),
            pltpu.SemaphoreType.DMA((36 + 2 * len(TWICE) + batch.bit_length() + len(SPANS) + len(PIECES),)),
        ],
        compiler_params=pltpu.CompilerParams(
            collective_id=0, has_side_effects=True, vmem_limit_bytes=56 * 1024 * 1024
        ),
        cost_estimate=pl.CostEstimate(
            flops=11_000_000_000, bytes_accessed=20_000_000, transcendentals=4_000_000
        ),
    )(
        lengths,
        tokens.reshape(4, 256, 768),
        w_query.T,
        w_key.T,
        w_value.T,
        w_out.reshape(1, 192, 768),
        w_up.reshape(4, 192, 768),
        w_down.reshape(4, 192, 768),
        down_query.T,
        down_value.T,
        up_query,
        up_value,
        gain_attn,
        gain_ffn,
        cotangent.reshape(4, 256, 768),
    )
    rows = jax.ShapeDtypeStruct((4, 256, 768), BF16)
    small = jax.ShapeDtypeStruct((8, 192), F32)
    activations, input_grad, grad_b_query, grad_b_value = pl.pallas_call(
        hand_over,
        out_shape=(rows, rows, small, small),
        in_specs=[anywhere] * 3,
        out_specs=[in_hbm] * 4,
        scratch_shapes=[pltpu.SemaphoreType.DMA((4,))],
        compiler_params=pltpu.CompilerParams(vmem_limit_bytes=1024 * 1024),
    )(*results)
    return (
        activations.reshape(tokens.shape),
        input_grad.reshape(tokens.shape),
        grad_b_query,
        grad_b_value,
    )


def solution(mesh):
    batch = mesh.shape["batch"]
    in_specs = (
        P("batch", None),
        P("batch"),
        P(None, "head"),
        P(None, "head"),
        P(None, "head"),
        P("head", None),
        P(),
        P(),
        P(None, "head"),
        P(None, "head"),
        P(None, "head"),
        P("head", None),
        P(),
        P(),
        P("batch", None),
    )
    out_specs = (P("batch", None), P("batch", None), P(None, "head"), P(None, "head"))
    return jax.shard_map(
        functools.partial(body, batch),
        mesh=mesh,
        in_specs=in_specs,
        out_specs=out_specs,
        check_vma=False,
    )
```

```python
import functools

import jax
import jax.numpy as jnp
from jax import lax
from jax.experimental import pallas as pl
from jax.experimental.pallas import tpu as pltpu
from jax.sharding import PartitionSpec as P

HD = 64
BF16 = jnp.bfloat16
F32 = jnp.float32
MESH = pl.DeviceIdType.MESH

OUT, UP, DOWN, QKV, ADAPTER = 0, 1, 5, 9, 12
ITEMS = 12
OWN, SIB, FAR, FARSIB = 0, 1, 2, 3
OVER_Y = (16, 0, 0, 0, 0, 32, 32, 32, 32, 32, 32, 32)
TWICE = (1, 2, 3, 4)
GROUPS = ((0, 1), (1, 2), (3, 2), (5, 2), (7, 1), (8, 1), (9, 3))
SPANS = ((0, 128), (128, 256), (384, 384))
PIECES = (
    (0, 256, 0, 128),
    (0, 256, 128, 256),
    (0, 256, 384, 256),
    (0, 128, 640, 128),
    (128, 128, 640, 128),
)
SEND_GROUPS = ("y", "x", "z", "t", "d", "c", "w", "ctx", "dctx", "rows", "b", "l", "g")


def dot(left, right, left_dim=1, right_dim=0):
    return lax.dot_general(
        left, right, (((left_dim,), (right_dim,)), ((), ())), preferred_element_type=F32
    )


def norm(z):
    centre = z - jnp.mean(z, axis=-1, keepdims=True)
    inverse = lax.rsqrt(jnp.mean(centre * centre, axis=-1, keepdims=True) + 1e-05)
    return centre * inverse, inverse


def norm_back(scaled, normed, inverse):
    return inverse * (
        scaled
        - jnp.mean(scaled, axis=-1, keepdims=True)
        - normed * jnp.mean(scaled * normed, axis=-1, keepdims=True)
    )


def flip(index, bit):
    return index + bit - 2 * bit * ((index // bit) % 2)


def kernel(
    batch,
    lengths,
    tokens,
    w_query,
    w_key,
    w_value,
    w_out,
    w_up,
    w_down,
    down_query,
    down_value,
    up_query,
    up_value,
    gain_one,
    gain_two,
    cotangent,
    activations,
    input_grad,
    grads_out,
    x,
    w,
    raw_down,
    raw_up,
    gains,
    cot,
    adapter_up,
    low,
    qkv,
    probs,
    log_sum,
    ctx_out,
    ctx_in,
    normed_one,
    inverse_one,
    hidden,
    hidden_low,
    act,
    slope,
    total,
    grad_z1,
    input_sum,
    dctx_out,
    dctx_in,
    grad_qkv,
    part_out,
    part_in,
    grads,
    grads_in,
    grads_all,
    grads_sums,
    local_sem,
    send_sem,
    recv_sem,
):
    b = lax.axis_index("batch")
    h = lax.axis_index("head")
    core = h % 2
    seq = h // 2
    far_seq = 1 - seq
    part = b % 4
    sibling = (b, flip(h, 1))
    across = (b, flip(h, 2))
    diagonal = (b, 3 - h)
    x_peer = (flip(b, 1), h)
    z_peer = (flip(b, 2), h)
    xz_peer = (flip(flip(b, 1), 2), h)
    batch_peers = [(flip(b, 1 << s), h) for s in range(2, batch.bit_length() - 1)]

    barrier = pltpu.get_barrier_semaphore()
    peers = [sibling, across, diagonal, x_peer, z_peer, xz_peer] + batch_peers
    for peer in peers:
        pl.semaphore_signal(barrier, inc=1, device_id=peer, device_id_type=MESH)

    recv_numbers = {}
    local_numbers = {}

    def copy(group, key, source, target, device):
        number = recv_numbers.setdefault(key, len(recv_numbers))
        return pltpu.make_async_remote_copy(
            src_ref=source,
            dst_ref=target,
            send_sem=send_sem.at[SEND_GROUPS.index(group)],
            recv_sem=recv_sem.at[number],
            device_id=device,
            device_id_type=MESH,
        )

    def send(group, key, source, target, device):
        copy(group, key, source, target, device).start()

    def arrived(key, target):
        copy("y", key, target, target, sibling).wait_recv()

    def sent(group, ref):
        copy(group, ("y", 0), ref, ref, sibling).wait_send()

    def local(key, source, target):
        number = local_numbers.setdefault(key, len(local_numbers))
        return pltpu.make_async_copy(source, target, local_sem.at[number])

    def load(key, source, target):
        local(key, source, target).start()

    def loaded(key, target):
        local(key, target, target).wait()

    for j, ref in enumerate((w_query, w_key, w_value)):
        load("qkv", ref, w.at[OWN, QKV + j])
    load("far", tokens.at[pl.ds(2 * far_seq, 2)], x.at[pl.ds(2 * far_seq, 2)])
    load("downs", down_query, raw_down.at[0])
    load("downs", down_value, raw_down.at[1])
    load("ups", up_query, raw_up.at[0])
    load("ups", up_value, raw_up.at[1])
    load("own", tokens.at[pl.ds(2 * seq, 2)], x.at[pl.ds(2 * seq, 2)])
    load("w", w_out, w.at[OWN, pl.ds(OUT, 1)])
    load("w", w_up, w.at[OWN, pl.ds(UP, 4)])
    load("w", w_down, w.at[OWN, pl.ds(DOWN, 4)])
    load("one", gain_one, gains.at[0])
    load("two", gain_two, gains.at[1])
    load("cot", cotangent.at[h], cot)

    far = w.at[FAR]
    px, pz, pd = flip(part, 1), flip(part, 2), 3 - part
    group_of = {}
    for first, count in GROUPS:
        for item in range(first, first + count):
            group_of[item] = first

    def rows_of(ref, item, index, start=0, count=48):
        return ref.at[item, pl.ds(pl.multiple_of(48 * index + start, 16), count)]

    def source_of(item):
        if item >= QKV:
            return w.at[OWN], item
        if item >= DOWN:
            return w_down, item - DOWN
        if item >= UP:
            return w_up, item - UP
        return w_out, item

    def send_part(*items):
        for item in items:
            source, at = source_of(item)
            mine, theirs = rows_of(source, at, part), rows_of(far, item, part)
            send("y", ("y", item), mine, theirs, across)

    def send_rest(*items):
        for item in items:
            source, at = source_of(item)
            count = OVER_Y[item]
            mine, theirs = rows_of(source, at, pd, 0, count), rows_of(far, item, pd, 0, count)
            send("t", ("f", group_of[item]), mine, theirs, across)

    def relay(*items):
        for item in items:
            mine = rows_of(far, item, part)
            arrived(("y", item), mine)
            twice = item in TWICE
            key = ("f", group_of[item])
            send("x", ("x", item) if twice else key, mine, mine, x_peer)
            send("z", ("z", item) if twice else key, mine, mine, z_peer)
            if not twice:
                count = OVER_Y[item]
                rest = rows_of(far, item, part, count, 48 - count)
                send("d", key, rest, rest, xz_peer)

    def relay_again(*items):
        for item in items:
            key = ("f", group_of[item])
            arrived(("x", item), rows_of(far, item, px))
            over_x = 32 if item % 2 else 16
            piece = rows_of(far, item, px, over_x, 48 - over_x)
            send("z", key, piece, piece, z_peer)
            arrived(("z", item), rows_of(far, item, pz))
            piece = rows_of(far, item, pz, 0, over_x)
            send("x", key, piece, piece, x_peer)

    def collect(group):
        first, count = GROUPS[group]
        items = pl.ds(first, count)
        arrived(("f", first), w.at[FAR, items, pl.ds(0, 48 if first in TWICE else 144)])
        if first < QKV:
            send("c", ("c", first), w.at[FAR, items], w.at[FARSIB, items], sibling)

    def collect_sibling(group):
        first, count = GROUPS[group]
        arrived(("c", first), w.at[FARSIB, pl.ds(first, count)])

    pl.semaphore_wait(barrier, len(peers))
    send_part(0)
    send_part(1)
    send_rest(0)
    send_part(2)
    send_part(3)
    send_part(4)
    send_part(5)
    send_part(6)
    pl.when(core == 1)(lambda: send_part(7))
    send("w", "so", w_out, w.at[SIB, pl.ds(OUT, 1)], sibling)
    send("w", "su", w_up, w.at[SIB, pl.ds(UP, 4)], sibling)
    send("w", "sd", w_down, w.at[SIB, pl.ds(DOWN, 4)], sibling)

    loaded("downs", raw_down)
    loaded("ups", raw_up)
    downs = jnp.concatenate([raw_down[0].astype(F32), raw_down[1].astype(F32)] * 2, axis=0)
    w[OWN, ADAPTER, :32] = downs.astype(BF16)
    w[FAR, ADAPTER, :32] = downs.astype(BF16)
    nothing = jnp.zeros((8, 192), F32)
    adapter_up[0, :, :192] = jnp.concatenate([raw_up[0].astype(F32), nothing], axis=0)
    adapter_up[0, :, 192:384] = jnp.zeros((16, 192), F32)
    adapter_up[0, :, 384:] = jnp.concatenate([nothing, raw_up[1].astype(F32)], axis=0)

    def adapted(slot, count):
        return w[slot, QKV:].reshape(768, 768)[:count]

    def project(rows, which, slot, store):
        full = dot(adapted(slot, 592), x[pl.ds(2 * rows, 2)].reshape(512, 768), 1, 1)
        lows = full[576:].astype(BF16)
        ups = adapter_up[0 if slot == OWN else 1].astype(BF16)
        if store:
            low[...] = lows
        query = full[:192] + 2.0 * dot(ups[:, :192], lows, 0, 0)
        value = full[384:576] + 2.0 * dot(ups[:, 384:], lows, 0, 0)
        qkv[which, :192] = query.astype(BF16)
        qkv[which, 192:384] = full[192:384].astype(BF16)
        qkv[which, 384:] = value.astype(BF16)

    def head_rows(j, head):
        return slice(192 * j + HD * head, 192 * j + HD * (head + 1))

    def scores_of(rows, which, head):
        position = lax.broadcasted_iota(jnp.int32, (512, 1), 0)
        bias = jnp.where(position < lengths[rows], 0.0, -1e30)
        query = qkv[which, head_rows(0, head)] * jnp.asarray(0.125, BF16)
        return dot(qkv[which, head_rows(1, head)], query, 0, 0) + bias

    def attend(rows, which, context):
        for head in range(3):
            scores = scores_of(rows, which, head)
            top = jnp.max(scores, axis=0, keepdims=True)
            exponent = jnp.exp(scores - top)
            amount = jnp.sum(exponent, axis=0, keepdims=True)
            probs[which, head] = (exponent * (1.0 / amount)).astype(BF16)
            if which == 1:
                log_sum[0, head] = top + jnp.log(amount)
        for head in range(3):
            out = dot(qkv[which, head_rows(2, head)], probs[which, head]).astype(BF16)
            ctx_out[context, 0, head_rows(0, head)] = out[:, :256]
            ctx_out[context, 1, head_rows(0, head)] = out[:, 256:]

    loaded("qkv", w.at[OWN, pl.ds(QKV, 3)])
    loaded("far", x.at[pl.ds(2 * far_seq, 2)])
    project(far_seq, 1, OWN, False)
    attend(far_seq, 1, 1)
    send("ctx", "ctx", ctx_out.at[1, core], ctx_in.at[FAR], across)
    send("ctx", "ctx", ctx_out.at[1, 1 - core], ctx_in.at[FARSIB], diagonal)
    pl.when(core == 0)(lambda: send_part(7))
    send_part(8)
    send_rest(5)
    send_rest(6)
    send_rest(7)
    send_rest(8)
    send_part(9)
    send_part(10)
    send_part(11)
    send_rest(9)
    send_rest(10)
    send_rest(11)
    send("b", "b", adapter_up.at[0], adapter_up.at[1], across)
    send("l", "l", log_sum.at[0], log_sum.at[1], across)
    relay(0)
    loaded("own", x.at[pl.ds(2 * seq, 2)])
    project(seq, 0, OWN, True)
    relay(1)
    attend(seq, 0, 0)
    send("ctx", "ctx", ctx_out.at[0, 1 - core], ctx_in.at[SIB], sibling)
    ctx_in[OWN] = ctx_out[0, core]
    relay(2)
    relay(3)
    relay_again(1)
    relay(4)
    relay_again(2)
    relay(5)
    collect(0)
    relay_again(3)
    relay(6)
    relay_again(4)
    pl.when(core == 1)(lambda: relay(7))

    loaded("w", w.at[OWN, pl.ds(0, QKV)])
    loaded("one", gains.at[0])
    loaded("two", gains.at[1])
    loaded("cot", cot)
    arrived("so", w.at[SIB, pl.ds(OUT, 1)])
    collect_sibling(0)
    arrived("ctx", ctx_in.at[pl.ds(1, 3)])
    attn = dot(ctx_in[...].reshape(768, 256), w[:, OUT].reshape(768, 768), 0, 0)
    n1, r1 = norm(x[h].astype(F32) + attn)
    normed_one[...] = n1
    inverse_one[...] = r1
    h1 = n1 * gains[0:1]
    hidden[...] = h1
    hidden_low[...] = h1.astype(BF16)

    def go_up(slot):
        up = dot(hidden_low[...], w[slot, UP : UP + 4].reshape(768, 768))
        phi = 0.5 * (1.0 + lax.erf(up * 0.7071067811865476))
        slope[slot] = phi + up * (0.3989422804014327 * jnp.exp(-0.5 * up * up))
        act[slot] = (up * phi).astype(BF16)

    def go_down(slot, first=0, count=4):
        rows = slice(192 * first, 192 * (first + count))
        weights = w[slot, DOWN + first : DOWN + first + count].reshape(192 * count, 768)
        return dot(act[slot, :, rows], weights)

    pl.when(core == 1)(lambda: relay(8))
    go_up(OWN)
    pl.when(core == 0)(lambda: relay(7))
    arrived("su", w.at[SIB, pl.ds(UP, 4)])
    go_up(SIB)
    arrived("sd", w.at[SIB, pl.ds(DOWN, 4)])
    total[...] = hidden[...] + go_down(OWN) + go_down(SIB)
    pl.when(core == 0)(lambda: relay(8))
    collect(1)
    collect(2)
    go_up(FAR)
    collect_sibling(1)
    collect_sibling(2)
    go_up(FARSIB)
    collect(3)
    collect(4)
    collect(5)
    total[...] += go_down(FAR, 0, 3)
    collect_sibling(3)
    collect_sibling(4)
    total[...] += go_down(FARSIB, 0, 3)
    total[...] += go_down(FAR, 3, 1)
    relay(9)
    collect_sibling(5)
    z2 = total[...] + go_down(FARSIB, 3, 1)

    n2, r2 = norm(z2)
    position = lax.broadcasted_iota(jnp.int32, (256, 1), 0) + 256 * core
    valid = (position < lengths[seq]).astype(F32)
    activations[h] = (valid * (n2 * gains[1:2])).astype(BF16)
    send("rows", "ay", activations.at[h], activations.at[h], across)
    send("rows", "all", activations.at[h], activations.at[h], sibling)
    d_z2 = norm_back(cot[...].astype(F32) * valid * gains[1:2], n2, r2)
    d_z2_low = d_z2.astype(BF16)
    relay(10)

    steps = []
    for slot in range(4):
        d_act = dot(d_z2_low, w[slot, DOWN : DOWN + 4].reshape(768, 768), 1, 1)
        steps.append((d_act * slope[slot]).astype(BF16))
    relay(11)
    grad_h1 = d_z2
    for slot in range(4):
        grad_h1 = grad_h1 + dot(steps[slot], w[slot, UP : UP + 4].reshape(768, 768), 1, 1)

    d_z1 = norm_back(grad_h1 * gains[0:1], normed_one[...], inverse_one[...])
    grad_z1[...] = d_z1
    d_z1_low = d_z1.astype(BF16)

    def d_context(first):
        pair = [w[first, OUT], w[first + 2, OUT]]
        d_ctx = dot(jnp.concatenate(pair, axis=0), d_z1_low, 1, 1).astype(BF16)
        dctx_out[first] = d_ctx[:192]
        dctx_out[first + 2] = d_ctx[192:]

    d_context(SIB)
    send("dctx", "dctx", dctx_out.at[SIB], dctx_in.at[core, 0], sibling)
    send("dctx", "dctx", dctx_out.at[FARSIB], dctx_in.at[core, 1], sibling)
    d_context(OWN)
    dctx_in[core, 0] = dctx_out[OWN]
    dctx_in[core, 1] = dctx_out[FAR]
    arrived("dctx", dctx_in.at[1 - core])

    def attend_back(which):
        d_scores = []
        for head in range(3):
            rows = head_rows(0, head)
            d_out = jnp.concatenate([dctx_in[0, which, rows], dctx_in[1, which, rows]], axis=1)
            if which == 0:
                probability = probs[0, head].astype(F32)
            else:
                probability = jnp.exp(scores_of(seq, 1, head) - log_sum[1, head])
                probs[1, head] = probability.astype(BF16)
            d_weights = dot(qkv[which, head_rows(2, head)], d_out, 0, 0)
            mean = jnp.sum(probability * d_weights, axis=0, keepdims=True)
            d_scores.append((probability * (d_weights - mean)).astype(BF16))
        for head in range(3):
            rows = head_rows(0, head)
            d_out = jnp.concatenate([dctx_in[0, which, rows], dctx_in[1, which, rows]], axis=1)
            d_query = (0.125 * dot(qkv[which, head_rows(1, head)], d_scores[head])).astype(BF16)
            d_key = 0.125 * dot(d_scores[head], qkv[which, head_rows(0, head)], 1, 1)
            d_value = dot(probs[which, head], d_out, 1, 1)
            pieces = (d_query, d_key.astype(BF16).T, d_value.astype(BF16).T)
            for j, piece in enumerate(pieces):
                grad_qkv[which, head_rows(j, head)] = piece

    def adapter_grads(which):
        for j in range(2):
            rows = slice(384 * j, 384 * j + 192)
            both = dot(low[...], grad_qkv[which, rows], 1, 1)
            grads[which, j] = 2.0 * both[8 * j : 8 * j + 8]

    def adapter_rows(which):
        d_low = 2.0 * dot(adapter_up[which].astype(BF16), grad_qkv[which, :576])
        coarse = d_low.astype(BF16)
        fine = (d_low - coarse.astype(F32)).astype(BF16)
        grad_qkv[which, 576:] = jnp.concatenate([coarse, fine], axis=0)

    def input_part(which, columns, half=None):
        weights = w[OWN if which == 0 else FAR, QKV:].reshape(768, 768)[:608, columns]
        if half is None:
            return dot(grad_qkv[which], weights, 0, 0).reshape(2, 256, 768)
        rows = pl.ds(pl.multiple_of(256 * half, 256), 256)
        return dot(grad_qkv[which, :, rows], weights, 0, 0)

    attend_back(0)
    adapter_rows(0)
    input_sum[...] = input_part(0, slice(0, 768))
    input_sum[core] += grad_z1[...]
    adapter_grads(0)

    collect(6)
    arrived("b", adapter_up.at[1])
    arrived("l", log_sum.at[1])
    project(seq, 1, FAR, False)
    attend_back(1)
    adapter_rows(1)
    spans = [(t, slice(first, first + count)) for t, (first, count) in enumerate(SPANS)]
    for t, columns in spans:
        given = input_sum[1 - core, :, columns] + input_part(1, columns, 1 - core)
        part_out[:, columns] = given.astype(BF16)
        send("rows", ("p", t), part_out.at[:, columns], part_in.at[:, columns], sibling)
        if t == 0:
            adapter_grads(1)
            send("g", "g", grads.at[1], grads_in, across)
    def piece_of(rows, n):
        row, count, column, width = PIECES[n]
        return input_grad.at[rows, pl.ds(row, count), pl.ds(column, width)]

    for t, columns in spans:
        own = input_sum[core, :, columns] + input_part(1, columns, core)
        arrived(("p", t), part_in.at[:, columns])
        input_grad[h, :, columns] = (own + part_in[:, columns].astype(F32)).astype(BF16)
        for n, (row, rows, column, width) in enumerate(PIECES):
            if columns.start <= column < columns.stop:
                block = piece_of(h, n)
                send("rows", ("i", n), block, block, across)
                if n == len(PIECES) - 1:
                    send("rows", "all", block, block, diagonal)
    send("rows", "all", input_grad.at[h], input_grad.at[h], sibling)

    def pass_on(n):
        block = piece_of(flip(h, 2), n)
        arrived(("i", n), block)
        if n < len(PIECES) - 1:
            send("rows", "all", block, block, sibling)

    arrived("ay", activations.at[flip(h, 2)])
    send("rows", "all", activations.at[flip(h, 2)], activations.at[flip(h, 2)], sibling)
    arrived("g", grads_in)
    grads_all[part] = grads[0] + grads_in[...]
    for peer in (x_peer, z_peer, xz_peer):
        send("g", "sums", grads_all.at[part], grads_all.at[part], peer)
    pass_on(0)
    arrived("sums", grads_all.at[pl.ds(0, 3)])
    sums = (grads_all[0] + grads_all[1]) + (grads_all[2] + grads_all[3])
    for n, peer in enumerate(batch_peers):
        grads_sums[2 * n] = sums
        send("g", ("g", n), grads_sums.at[2 * n], grads_sums.at[2 * n + 1], peer)
        if n == 0:
            for m in range(1, len(PIECES)):
                pass_on(m)
        arrived(("g", n), grads_sums.at[2 * n + 1])
        sums = sums + grads_sums[2 * n + 1]
    grads_out[...] = sums
    for n in range(1, 1 if batch_peers else len(PIECES)):
        pass_on(n)
    arrived("all", activations)

    def rows_block(count):
        tiles = count // 16
        shapes = [(m, n, tiles // (m * n)) for m in (1, 2, 3, 4) for n in range(1, 13) if tiles % (m * n) == 0]
        inner, outer, depth = next(shape for shape in shapes if shape[2] <= 12)
        return w.at[pl.ds(0, inner), pl.ds(0, outer), pl.ds(0, 16 * depth)]

    sent("y", w.at[FAR, pl.ds(0, 3)])
    sent("x", rows_block(48 * ITEMS + 24 * len(TWICE)))
    sent("z", rows_block(48 * ITEMS + 24 * len(TWICE)))
    sent("t", rows_block(sum(OVER_Y)))
    sent("d", rows_block(sum(48 - OVER_Y[n] for n in range(ITEMS) if n not in TWICE)))
    sent("c", w.at[FAR, pl.ds(0, 9)])
    sent("w", w.at[SIB, pl.ds(0, 9)])
    sent("ctx", ctx_in.at[pl.ds(0, 3)])
    sent("dctx", dctx_in.at[0])
    sent("rows", w.at[pl.ds(0, 4), pl.ds(0, 7), pl.ds(0, 64)])
    sent("b", adapter_up.at[0])
    sent("l", log_sum.at[0])
    sent("g", grads_sums.at[pl.ds(0, 4 + len(batch_peers))])


def hand_over(activations, input_grad, grads, *rest):
    targets, sem = rest[:4], rest[4]
    sources = (activations, input_grad, grads.at[0], grads.at[1])
    copies = [
        pltpu.make_async_copy(source, target, sem.at[n])
        for n, (source, target) in enumerate(zip(sources, targets))
    ]
    for c in copies:
        c.start()
    for c in copies:
        c.wait()


def body(batch, *given):
    (
        tokens,
        lengths,
        w_query,
        w_key,
        w_value,
        w_out,
        down_query,
        down_value,
        up_query,
        up_value,
        w_up,
        w_down,
        gain_attn,
        gain_ffn,
        cotangent,
    ) = given
    anywhere = pl.BlockSpec(memory_space=pl.ANY)
    in_vmem = pl.BlockSpec(memory_space=pltpu.VMEM)
    in_hbm = pl.BlockSpec(memory_space=pltpu.HBM)
    vmem = pltpu.VMEM
    results = pl.pallas_call(
        functools.partial(kernel, batch),
        out_shape=(
            vmem((4, 256, 768), BF16),
            vmem((4, 256, 768), BF16),
            vmem((2, 8, 192), F32),
        ),
        in_specs=[pl.BlockSpec(memory_space=pltpu.SMEM)] + [in_hbm] * 14,
        out_specs=(in_vmem,) * 3,
        scratch_shapes=[
            vmem((4, 256, 768), BF16),
            vmem((4, 13, 192, 768), BF16),
            vmem((2, 8, 768), BF16),
            vmem((2, 8, 192), BF16),
            vmem((2, 768), F32),
            vmem((256, 768), BF16),
            vmem((2, 16, 576), F32),
            vmem((16, 512), BF16),
            vmem((2, 576, 512), BF16),
            vmem((2, 3, 512, 512), BF16),
            vmem((2, 3, 1, 512), F32),
            vmem((2, 2, 192, 256), BF16),
            vmem((4, 192, 256), BF16),
            vmem((256, 768), F32),
            vmem((256, 1), F32),
            vmem((256, 768), F32),
            vmem((256, 768), BF16),
            vmem((4, 256, 768), BF16),
            vmem((4, 256, 768), F32),
            vmem((256, 768), F32),
            vmem((256, 768), F32),
            vmem((2, 256, 768), F32),
            vmem((4, 192, 256), BF16),
            vmem((2, 2, 192, 256), BF16),
            vmem((2, 608, 512), BF16),
            vmem((256, 768), BF16),
            vmem((256, 768), BF16),
            vmem((2, 2, 8, 192), F32),
            vmem((2, 8, 192), F32),
            vmem((4, 2, 8, 192), F32),
            vmem((2 * batch.bit_length(), 2, 8, 192), F32),
            pltpu.SemaphoreType.DMA((9,)),
            pltpu.SemaphoreType.DMA((len(SEND_GROUPS),)),
            pltpu.SemaphoreType.DMA((36 + 2 * len(TWICE) + batch.bit_length() + len(SPANS) + len(PIECES),)),
        ],
        compiler_params=pltpu.CompilerParams(
            collective_id=0, has_side_effects=True, vmem_limit_bytes=56 * 1024 * 1024
        ),
        cost_estimate=pl.CostEstimate(
            flops=11_000_000_000, bytes_accessed=20_000_000, transcendentals=4_000_000
        ),
    )(
        lengths,
        tokens.reshape(4, 256, 768),
        w_query.T,
        w_key.T,
        w_value.T,
        w_out.reshape(1, 192, 768),
        w_up.reshape(4, 192, 768),
        w_down.reshape(4, 192, 768),
        down_query.T,
        down_value.T,
        up_query,
        up_value,
        gain_attn,
        gain_ffn,
        cotangent.reshape(4, 256, 768),
    )
    rows = jax.ShapeDtypeStruct((4, 256, 768), BF16)
    small = jax.ShapeDtypeStruct((8, 192), F32)
    activations, input_grad, grad_b_query, grad_b_value = pl.pallas_call(
        hand_over,
        out_shape=(rows, rows, small, small),
        in_specs=[anywhere] * 3,
        out_specs=[in_hbm] * 4,
        scratch_shapes=[pltpu.SemaphoreType.DMA((4,))],
        compiler_params=pltpu.CompilerParams(vmem_limit_bytes=1024 * 1024),
    )(*results)
    return (
        activations.reshape(tokens.shape),
        input_grad.reshape(tokens.shape),
        grad_b_query,
        grad_b_value,
    )


def solution(mesh):
    batch = mesh.shape["batch"]
    in_specs = (
        P("batch", None),
        P("batch"),
        P(None, "head"),
        P(None, "head"),
        P(None, "head"),
        P("head", None),
        P(),
        P(),
        P(None, "head"),
        P(None, "head"),
        P(None, "head"),
        P("head", None),
        P(),
        P(),
        P("batch", None),
    )
    out_specs = (P("batch", None), P("batch", None), P(None, "head"), P(None, "head"))
    return jax.shard_map(
        functools.partial(body, batch),
        mesh=mesh,
        in_specs=in_specs,
        out_specs=out_specs,
        check_vma=False,
    )
```

```python
import functools

import jax
import jax.numpy as jnp
from jax import lax
from jax.experimental import pallas as pl
from jax.experimental.pallas import tpu as pltpu
from jax.sharding import PartitionSpec as P

HD = 64
BF16 = jnp.bfloat16
F32 = jnp.float32
MESH = pl.DeviceIdType.MESH

OUT, UP, DOWN, QKV, ADAPTER = 0, 1, 5, 9, 12
ITEMS = 12
OWN, SIB, FAR, FARSIB = 0, 1, 2, 3
OVER_Y = (16, 0, 0, 0, 0, 32, 32, 32, 32, 32, 32, 32)
TWICE = (1, 2, 3, 4)
GROUPS = ((0, 1), (1, 2), (3, 2), (5, 2), (7, 1), (8, 1), (9, 3))
SPANS = ((0, 128), (128, 256), (384, 384))
PIECES = (
    (0, 256, 0, 128),
    (0, 256, 128, 256),
    (0, 256, 384, 256),
    (0, 128, 640, 128),
    (128, 128, 640, 128),
)
SEND_GROUPS = ("y", "x", "z", "t", "d", "c", "w", "ctx", "dctx", "rows", "b", "l", "g")


def dot(left, right, left_dim=1, right_dim=0):
    return lax.dot_general(
        left, right, (((left_dim,), (right_dim,)), ((), ())), preferred_element_type=F32
    )


def norm(z):
    centre = z - jnp.mean(z, axis=-1, keepdims=True)
    inverse = lax.rsqrt(jnp.mean(centre * centre, axis=-1, keepdims=True) + 1e-05)
    return centre * inverse, inverse


def norm_back(scaled, normed, inverse):
    return inverse * (
        scaled
        - jnp.mean(scaled, axis=-1, keepdims=True)
        - normed * jnp.mean(scaled * normed, axis=-1, keepdims=True)
    )


def flip(index, bit):
    return index + bit - 2 * bit * ((index // bit) % 2)


def kernel(
    batch,
    lengths,
    tokens,
    w_query,
    w_key,
    w_value,
    w_out,
    w_up,
    w_down,
    down_query,
    down_value,
    up_query,
    up_value,
    gain_one,
    gain_two,
    cotangent,
    activations,
    input_grad,
    grads_out,
    x,
    w,
    raw_down,
    raw_up,
    gains,
    cot,
    adapter_up,
    ups_out,
    low,
    qkv,
    probs,
    log_sum,
    ctx_out,
    ctx_in,
    normed_one,
    inverse_one,
    hidden,
    hidden_low,
    act,
    slope,
    total,
    grad_z1,
    input_sum,
    dctx_out,
    dctx_in,
    grad_qkv,
    part_out,
    part_in,
    grads,
    grads_in,
    grads_all,
    grads_sums,
    local_sem,
    send_sem,
    recv_sem,
):
    b = lax.axis_index("batch")
    h = lax.axis_index("head")
    core = h % 2
    seq = h // 2
    far_seq = 1 - seq
    part = b % 4
    sibling = (b, flip(h, 1))
    across = (b, flip(h, 2))
    diagonal = (b, 3 - h)
    x_peer = (flip(b, 1), h)
    z_peer = (flip(b, 2), h)
    xz_peer = (flip(flip(b, 1), 2), h)
    batch_peers = [(flip(b, 1 << s), h) for s in range(2, batch.bit_length() - 1)]

    barrier = pltpu.get_barrier_semaphore()
    peers = [sibling, across, diagonal, x_peer, z_peer, xz_peer] + batch_peers
    for peer in peers:
        pl.semaphore_signal(barrier, inc=1, device_id=peer, device_id_type=MESH)

    recv_numbers = {}
    local_numbers = {}

    def copy(group, key, source, target, device):
        number = recv_numbers.setdefault(key, len(recv_numbers))
        return pltpu.make_async_remote_copy(
            src_ref=source,
            dst_ref=target,
            send_sem=send_sem.at[SEND_GROUPS.index(group)],
            recv_sem=recv_sem.at[number],
            device_id=device,
            device_id_type=MESH,
        )

    def send(group, key, source, target, device):
        copy(group, key, source, target, device).start()

    def arrived(key, target):
        copy("y", key, target, target, sibling).wait_recv()

    def sent(group, ref):
        copy(group, ("y", 0), ref, ref, sibling).wait_send()

    def local(key, source, target):
        number = local_numbers.setdefault(key, len(local_numbers))
        return pltpu.make_async_copy(source, target, local_sem.at[number])

    def load(key, source, target):
        local(key, source, target).start()

    def loaded(key, target):
        local(key, target, target).wait()

    for j, ref in enumerate((w_query, w_key, w_value)):
        load("qkv", ref, w.at[OWN, QKV + j])
    load("far", tokens.at[pl.ds(2 * far_seq, 2)], x.at[pl.ds(2 * far_seq, 2)])
    load("downs", down_query, raw_down.at[0])
    load("downs", down_value, raw_down.at[1])
    load("ups", up_query, raw_up.at[0])
    load("ups", up_value, raw_up.at[1])
    load("own", tokens.at[pl.ds(2 * seq, 2)], x.at[pl.ds(2 * seq, 2)])
    load("w", w_out, w.at[OWN, pl.ds(OUT, 1)])
    load("w", w_up, w.at[OWN, pl.ds(UP, 4)])
    load("w", w_down, w.at[OWN, pl.ds(DOWN, 4)])
    load("one", gain_one, gains.at[0])
    load("two", gain_two, gains.at[1])
    load("cot", cotangent.at[h], cot)

    far = w.at[FAR]
    px, pz, pd = flip(part, 1), flip(part, 2), 3 - part
    group_of = {}
    for first, count in GROUPS:
        for item in range(first, first + count):
            group_of[item] = first

    def rows_of(ref, item, index, start=0, count=48):
        return ref.at[item, pl.ds(pl.multiple_of(48 * index + start, 16), count)]

    def source_of(item):
        if item >= QKV:
            return w.at[OWN], item
        if item >= DOWN:
            return w_down, item - DOWN
        if item >= UP:
            return w_up, item - UP
        return w_out, item

    def send_part(*items):
        for item in items:
            source, at = source_of(item)
            mine, theirs = rows_of(source, at, part), rows_of(far, item, part)
            send("y", ("y", item), mine, theirs, across)

    def send_rest(*items):
        for item in items:
            source, at = source_of(item)
            count = OVER_Y[item]
            mine, theirs = rows_of(source, at, pd, 0, count), rows_of(far, item, pd, 0, count)
            send("t", ("f", group_of[item]), mine, theirs, across)

    def relay(*items):
        for item in items:
            mine = rows_of(far, item, part)
            arrived(("y", item), mine)
            twice = item in TWICE
            key = ("f", group_of[item])
            send("x", ("x", item) if twice else key, mine, mine, x_peer)
            send("z", ("z", item) if twice else key, mine, mine, z_peer)
            if not twice:
                count = OVER_Y[item]
                rest = rows_of(far, item, part, count, 48 - count)
                send("d", key, rest, rest, xz_peer)

    def relay_again(*items):
        for item in items:
            key = ("f", group_of[item])
            arrived(("x", item), rows_of(far, item, px))
            over_x = 32 if item % 2 else 16
            piece = rows_of(far, item, px, over_x, 48 - over_x)
            send("z", key, piece, piece, z_peer)
            arrived(("z", item), rows_of(far, item, pz))
            piece = rows_of(far, item, pz, 0, over_x)
            send("x", key, piece, piece, x_peer)

    def collect(group):
        first, count = GROUPS[group]
        items = pl.ds(first, count)
        arrived(("f", first), w.at[FAR, items, pl.ds(0, 48 if first in TWICE else 144)])
        if first < QKV:
            send("c", ("c", first), w.at[FAR, items], w.at[FARSIB, items], sibling)

    def collect_sibling(group):
        first, count = GROUPS[group]
        arrived(("c", first), w.at[FARSIB, pl.ds(first, count)])

    pl.semaphore_wait(barrier, len(peers))
    send_part(0)
    send_part(1)
    send_rest(0)
    send_part(2)
    send_part(3)
    send_part(4)
    send_part(5)
    send_part(6)
    pl.when(core == 1)(lambda: send_part(7))
    send("w", "so", w_out, w.at[SIB, pl.ds(OUT, 1)], sibling)
    send("w", "su", w_up, w.at[SIB, pl.ds(UP, 4)], sibling)
    send("w", "sd", w_down, w.at[SIB, pl.ds(DOWN, 4)], sibling)

    loaded("downs", raw_down)
    loaded("ups", raw_up)
    downs = jnp.concatenate([raw_down[0].astype(F32), raw_down[1].astype(F32)] * 2, axis=0)
    w[OWN, ADAPTER, :32] = downs.astype(BF16)
    w[FAR, ADAPTER, :32] = downs.astype(BF16)
    ups_out[0] = jnp.concatenate([raw_up[0].astype(F32), raw_up[1].astype(F32)], axis=0).astype(BF16)
    mine_up = lax.broadcasted_iota(jnp.int32, (16, 192), 0) < 8

    def spread_up(which):
        both = ups_out[which].astype(F32)
        adapter_up[which, :, :192] = jnp.where(mine_up, both, 0.0)
        adapter_up[which, :, 192:384] = jnp.zeros((16, 192), F32)
        adapter_up[which, :, 384:] = jnp.where(mine_up, 0.0, both)

    spread_up(0)

    def adapted(slot, count):
        return w[slot, QKV:].reshape(768, 768)[:count]

    def project(rows, which, slot, store):
        full = dot(adapted(slot, 592), x[pl.ds(2 * rows, 2)].reshape(512, 768), 1, 1)
        lows = full[576:].astype(BF16)
        ups = adapter_up[0 if slot == OWN else 1].astype(BF16)
        if store:
            low[...] = lows
        query = full[:192] + 2.0 * dot(ups[:, :192], lows, 0, 0)
        value = full[384:576] + 2.0 * dot(ups[:, 384:], lows, 0, 0)
        qkv[which, :192] = query.astype(BF16)
        qkv[which, 192:384] = full[192:384].astype(BF16)
        qkv[which, 384:] = value.astype(BF16)

    def head_rows(j, head):
        return slice(192 * j + HD * head, 192 * j + HD * (head + 1))

    def scores_of(rows, which, head):
        position = lax.broadcasted_iota(jnp.int32, (512, 1), 0)
        bias = jnp.where(position < lengths[rows], 0.0, -1e30)
        query = qkv[which, head_rows(0, head)] * jnp.asarray(0.125, BF16)
        return dot(qkv[which, head_rows(1, head)], query, 0, 0) + bias

    def attend(rows, which, context):
        for head in range(3):
            scores = scores_of(rows, which, head)
            top = jnp.max(scores, axis=0, keepdims=True)
            exponent = jnp.exp(scores - top)
            amount = jnp.sum(exponent, axis=0, keepdims=True)
            probs[which, head] = (exponent * (1.0 / amount)).astype(BF16)
            if which == 1:
                log_sum[0, head] = top + jnp.log(amount)
        for head in range(3):
            out = dot(qkv[which, head_rows(2, head)], probs[which, head]).astype(BF16)
            ctx_out[context, 0, head_rows(0, head)] = out[:, :256]
            ctx_out[context, 1, head_rows(0, head)] = out[:, 256:]

    loaded("qkv", w.at[OWN, pl.ds(QKV, 3)])
    loaded("far", x.at[pl.ds(2 * far_seq, 2)])
    project(far_seq, 1, OWN, False)
    attend(far_seq, 1, 1)
    send("ctx", "ctx", ctx_out.at[1, core], ctx_in.at[FAR], across)
    send("ctx", "ctx", ctx_out.at[1, 1 - core], ctx_in.at[FARSIB], diagonal)
    pl.when(core == 0)(lambda: send_part(7))
    send_part(8)
    send_rest(5)
    send_rest(6)
    send_rest(7)
    send_rest(8)
    send_part(9)
    send_part(10)
    send_part(11)
    send_rest(9)
    send_rest(10)
    send_rest(11)
    send("b", "b", ups_out.at[0], ups_out.at[1], across)
    send("l", "l", log_sum.at[0], log_sum.at[1], across)
    relay(0)
    loaded("own", x.at[pl.ds(2 * seq, 2)])
    project(seq, 0, OWN, True)
    relay(1)
    attend(seq, 0, 0)
    send("ctx", "ctx", ctx_out.at[0, 1 - core], ctx_in.at[SIB], sibling)
    ctx_in[OWN] = ctx_out[0, core]
    relay(2)
    relay(3)
    relay_again(1)
    relay(4)
    relay_again(2)
    relay(5)
    collect(0)
    relay_again(3)
    relay(6)
    relay_again(4)
    pl.when(core == 1)(lambda: relay(7))

    loaded("w", w.at[OWN, pl.ds(0, QKV)])
    loaded("one", gains.at[0])
    loaded("two", gains.at[1])
    loaded("cot", cot)
    arrived("so", w.at[SIB, pl.ds(OUT, 1)])
    collect_sibling(0)
    arrived("ctx", ctx_in.at[pl.ds(1, 3)])
    attn = dot(ctx_in[...].reshape(768, 256), w[:, OUT].reshape(768, 768), 0, 0)
    n1, r1 = norm(x[h].astype(F32) + attn)
    normed_one[...] = n1
    inverse_one[...] = r1
    h1 = n1 * gains[0:1]
    hidden[...] = h1
    hidden_low[...] = h1.astype(BF16)

    def go_up(slot):
        up = dot(hidden_low[...], w[slot, UP : UP + 4].reshape(768, 768))
        phi = 0.5 * (1.0 + lax.erf(up * 0.7071067811865476))
        slope[slot] = phi + up * (0.3989422804014327 * jnp.exp(-0.5 * up * up))
        act[slot] = (up * phi).astype(BF16)

    def go_down(slot, first=0, count=4):
        rows = slice(192 * first, 192 * (first + count))
        weights = w[slot, DOWN + first : DOWN + first + count].reshape(192 * count, 768)
        return dot(act[slot, :, rows], weights)

    pl.when(core == 1)(lambda: relay(8))
    go_up(OWN)
    pl.when(core == 0)(lambda: relay(7))
    arrived("su", w.at[SIB, pl.ds(UP, 4)])
    go_up(SIB)
    arrived("sd", w.at[SIB, pl.ds(DOWN, 4)])
    total[...] = hidden[...] + go_down(OWN) + go_down(SIB)
    pl.when(core == 0)(lambda: relay(8))
    collect(1)
    collect(2)
    go_up(FAR)
    collect_sibling(1)
    collect_sibling(2)
    go_up(FARSIB)
    collect(3)
    collect(4)
    collect(5)
    total[...] += go_down(FAR, 0, 3)
    collect_sibling(3)
    collect_sibling(4)
    total[...] += go_down(FARSIB, 0, 3)
    total[...] += go_down(FAR, 3, 1)
    relay(9)
    collect_sibling(5)
    z2 = total[...] + go_down(FARSIB, 3, 1)

    n2, r2 = norm(z2)
    position = lax.broadcasted_iota(jnp.int32, (256, 1), 0) + 256 * core
    valid = (position < lengths[seq]).astype(F32)
    activations[h] = (valid * (n2 * gains[1:2])).astype(BF16)
    send("rows", "ay", activations.at[h], activations.at[h], across)
    send("rows", "all", activations.at[h], activations.at[h], sibling)
    d_z2 = norm_back(cot[...].astype(F32) * valid * gains[1:2], n2, r2)
    d_z2_low = d_z2.astype(BF16)
    relay(10)

    steps = []
    for slot in range(4):
        d_act = dot(d_z2_low, w[slot, DOWN : DOWN + 4].reshape(768, 768), 1, 1)
        steps.append((d_act * slope[slot]).astype(BF16))
    grad_h1 = d_z2
    for slot in range(4):
        grad_h1 = grad_h1 + dot(steps[slot], w[slot, UP : UP + 4].reshape(768, 768), 1, 1)

    d_z1 = norm_back(grad_h1 * gains[0:1], normed_one[...], inverse_one[...])
    grad_z1[...] = d_z1
    d_z1_low = d_z1.astype(BF16)
    relay(11)

    def d_context(first):
        pair = [w[first, OUT], w[first + 2, OUT]]
        d_ctx = dot(jnp.concatenate(pair, axis=0), d_z1_low, 1, 1).astype(BF16)
        dctx_out[first] = d_ctx[:192]
        dctx_out[first + 2] = d_ctx[192:]

    d_context(SIB)
    send("dctx", "dctx", dctx_out.at[SIB], dctx_in.at[core, 0], sibling)
    send("dctx", "dctx", dctx_out.at[FARSIB], dctx_in.at[core, 1], sibling)
    d_context(OWN)
    dctx_in[core, 0] = dctx_out[OWN]
    dctx_in[core, 1] = dctx_out[FAR]
    arrived("dctx", dctx_in.at[1 - core])

    def attend_back(which):
        d_scores = []
        for head in range(3):
            rows = head_rows(0, head)
            d_out = jnp.concatenate([dctx_in[0, which, rows], dctx_in[1, which, rows]], axis=1)
            if which == 0:
                probability = probs[0, head].astype(F32)
            else:
                probability = jnp.exp(scores_of(seq, 1, head) - log_sum[1, head])
                probs[1, head] = probability.astype(BF16)
            d_weights = dot(qkv[which, head_rows(2, head)], d_out, 0, 0)
            mean = jnp.sum(probability * d_weights, axis=0, keepdims=True)
            d_scores.append((probability * (d_weights - mean)).astype(BF16))
        for head in range(3):
            rows = head_rows(0, head)
            d_out = jnp.concatenate([dctx_in[0, which, rows], dctx_in[1, which, rows]], axis=1)
            d_query = (0.125 * dot(qkv[which, head_rows(1, head)], d_scores[head])).astype(BF16)
            d_key = 0.125 * dot(d_scores[head], qkv[which, head_rows(0, head)], 1, 1)
            d_value = dot(probs[which, head], d_out, 1, 1)
            pieces = (d_query, d_key.astype(BF16).T, d_value.astype(BF16).T)
            for j, piece in enumerate(pieces):
                grad_qkv[which, head_rows(j, head)] = piece

    def adapter_grads(which):
        for j in range(2):
            rows = slice(384 * j, 384 * j + 192)
            both = dot(low[...], grad_qkv[which, rows], 1, 1)
            grads[which, j] = 2.0 * both[8 * j : 8 * j + 8]

    def adapter_rows(which):
        d_low = 2.0 * dot(adapter_up[which].astype(BF16), grad_qkv[which, :576])
        coarse = d_low.astype(BF16)
        fine = (d_low - coarse.astype(F32)).astype(BF16)
        grad_qkv[which, 576:] = jnp.concatenate([coarse, fine], axis=0)

    def input_part(which, columns, half=None):
        weights = w[OWN if which == 0 else FAR, QKV:].reshape(768, 768)[:608, columns]
        if half is None:
            return dot(grad_qkv[which], weights, 0, 0).reshape(2, 256, 768)
        rows = pl.ds(pl.multiple_of(256 * half, 256), 256)
        return dot(grad_qkv[which, :, rows], weights, 0, 0)

    attend_back(0)
    adapter_rows(0)
    input_sum[...] = input_part(0, slice(0, 768))
    input_sum[core] += grad_z1[...]
    adapter_grads(0)

    collect(6)
    arrived("b", ups_out.at[1])
    spread_up(1)
    arrived("l", log_sum.at[1])
    project(seq, 1, FAR, False)
    attend_back(1)
    adapter_rows(1)
    spans = [(t, slice(first, first + count)) for t, (first, count) in enumerate(SPANS)]
    def piece_of(rows, n):
        row, count, column, width = PIECES[n]
        return input_grad.at[rows, pl.ds(row, count), pl.ds(column, width)]

    def give(t):
        columns = spans[t][1]
        given = input_sum[1 - core, :, columns] + input_part(1, columns, 1 - core)
        part_out[:, columns] = given.astype(BF16)
        send("rows", ("p", t), part_out.at[:, columns], part_in.at[:, columns], sibling)

    def take(t):
        columns = spans[t][1]
        own = input_sum[core, :, columns] + input_part(1, columns, core)
        arrived(("p", t), part_in.at[:, columns])
        input_grad[h, :, columns] = (own + part_in[:, columns].astype(F32)).astype(BF16)
        for n, (row, rows, column, width) in enumerate(PIECES):
            if columns.start <= column < columns.stop:
                block = piece_of(h, n)
                send("rows", ("i", n), block, block, across)
                if n == len(PIECES) - 1:
                    send("rows", "all", block, block, diagonal)

    give(0)
    adapter_grads(1)
    send("g", "g", grads.at[1], grads_in, across)
    give(1)
    take(0)
    give(2)
    take(1)
    take(2)
    send("rows", "all", input_grad.at[h], input_grad.at[h], sibling)

    def pass_on(n):
        block = piece_of(flip(h, 2), n)
        arrived(("i", n), block)
        if n < len(PIECES) - 1:
            send("rows", "all", block, block, sibling)

    arrived("ay", activations.at[flip(h, 2)])
    send("rows", "all", activations.at[flip(h, 2)], activations.at[flip(h, 2)], sibling)
    arrived("g", grads_in)
    grads_all[part] = grads[0] + grads_in[...]
    for peer in (x_peer, z_peer, xz_peer):
        send("g", "sums", grads_all.at[part], grads_all.at[part], peer)
    pass_on(0)
    arrived("sums", grads_all.at[pl.ds(0, 3)])
    sums = (grads_all[0] + grads_all[1]) + (grads_all[2] + grads_all[3])
    for n, peer in enumerate(batch_peers):
        grads_sums[2 * n] = sums
        send("g", ("g", n), grads_sums.at[2 * n], grads_sums.at[2 * n + 1], peer)
        if n == 0:
            for m in range(1, len(PIECES)):
                pass_on(m)
        arrived(("g", n), grads_sums.at[2 * n + 1])
        sums = sums + grads_sums[2 * n + 1]
    grads_out[...] = sums
    for n in range(1, 1 if batch_peers else len(PIECES)):
        pass_on(n)
    arrived("all", activations)

    def rows_block(count):
        tiles = count // 16
        shapes = [(m, n, tiles // (m * n)) for m in (1, 2, 3, 4) for n in range(1, 13) if tiles % (m * n) == 0]
        inner, outer, depth = next(shape for shape in shapes if shape[2] <= 12)
        return w.at[pl.ds(0, inner), pl.ds(0, outer), pl.ds(0, 16 * depth)]

    sent("y", w.at[FAR, pl.ds(0, 3)])
    sent("x", rows_block(48 * ITEMS + 24 * len(TWICE)))
    sent("z", rows_block(48 * ITEMS + 24 * len(TWICE)))
    sent("t", rows_block(sum(OVER_Y)))
    sent("d", rows_block(sum(48 - OVER_Y[n] for n in range(ITEMS) if n not in TWICE)))
    sent("c", w.at[FAR, pl.ds(0, 9)])
    sent("w", w.at[SIB, pl.ds(0, 9)])
    sent("ctx", ctx_in.at[pl.ds(0, 3)])
    sent("dctx", dctx_in.at[0])
    sent("rows", w.at[pl.ds(0, 4), pl.ds(0, 7), pl.ds(0, 64)])
    sent("b", ups_out.at[0])
    sent("l", log_sum.at[0])
    sent("g", grads_sums.at[pl.ds(0, 4 + len(batch_peers))])


def hand_over(activations, input_grad, grads, *rest):
    targets, sem = rest[:4], rest[4]
    sources = (activations, input_grad, grads.at[0], grads.at[1])
    copies = [
        pltpu.make_async_copy(source, target, sem.at[n])
        for n, (source, target) in enumerate(zip(sources, targets))
    ]
    for c in copies:
        c.start()
    for c in copies:
        c.wait()


def body(batch, *given):
    (
        tokens,
        lengths,
        w_query,
        w_key,
        w_value,
        w_out,
        down_query,
        down_value,
        up_query,
        up_value,
        w_up,
        w_down,
        gain_attn,
        gain_ffn,
        cotangent,
    ) = given
    anywhere = pl.BlockSpec(memory_space=pl.ANY)
    in_vmem = pl.BlockSpec(memory_space=pltpu.VMEM)
    in_hbm = pl.BlockSpec(memory_space=pltpu.HBM)
    vmem = pltpu.VMEM
    results = pl.pallas_call(
        functools.partial(kernel, batch),
        out_shape=(
            vmem((4, 256, 768), BF16),
            vmem((4, 256, 768), BF16),
            vmem((2, 8, 192), F32),
        ),
        in_specs=[pl.BlockSpec(memory_space=pltpu.SMEM)] + [in_hbm] * 14,
        out_specs=(in_vmem,) * 3,
        scratch_shapes=[
            vmem((4, 256, 768), BF16),
            vmem((4, 13, 192, 768), BF16),
            vmem((2, 8, 768), BF16),
            vmem((2, 8, 192), BF16),
            vmem((2, 768), F32),
            vmem((256, 768), BF16),
            vmem((2, 16, 576), F32),
            vmem((2, 16, 192), BF16),
            vmem((16, 512), BF16),
            vmem((2, 576, 512), BF16),
            vmem((2, 3, 512, 512), BF16),
            vmem((2, 3, 1, 512), F32),
            vmem((2, 2, 192, 256), BF16),
            vmem((4, 192, 256), BF16),
            vmem((256, 768), F32),
            vmem((256, 1), F32),
            vmem((256, 768), F32),
            vmem((256, 768), BF16),
            vmem((4, 256, 768), BF16),
            vmem((4, 256, 768), F32),
            vmem((256, 768), F32),
            vmem((256, 768), F32),
            vmem((2, 256, 768), F32),
            vmem((4, 192, 256), BF16),
            vmem((2, 2, 192, 256), BF16),
            vmem((2, 608, 512), BF16),
            vmem((256, 768), BF16),
            vmem((256, 768), BF16),
            vmem((2, 2, 8, 192), F32),
            vmem((2, 8, 192), F32),
            vmem((4, 2, 8, 192), F32),
            vmem((2 * batch.bit_length(), 2, 8, 192), F32),
            pltpu.SemaphoreType.DMA((9,)),
            pltpu.SemaphoreType.DMA((len(SEND_GROUPS),)),
            pltpu.SemaphoreType.DMA((33 + 2 * len(TWICE) + batch.bit_length() + len(SPANS) + len(PIECES),)),
        ],
        compiler_params=pltpu.CompilerParams(
            collective_id=0, has_side_effects=True, vmem_limit_bytes=56 * 1024 * 1024
        ),
        cost_estimate=pl.CostEstimate(
            flops=11_000_000_000, bytes_accessed=20_000_000, transcendentals=4_000_000
        ),
    )(
        lengths,
        tokens.reshape(4, 256, 768),
        w_query.T,
        w_key.T,
        w_value.T,
        w_out.reshape(1, 192, 768),
        w_up.reshape(4, 192, 768),
        w_down.reshape(4, 192, 768),
        down_query.T,
        down_value.T,
        up_query,
        up_value,
        gain_attn,
        gain_ffn,
        cotangent.reshape(4, 256, 768),
    )
    rows = jax.ShapeDtypeStruct((4, 256, 768), BF16)
    small = jax.ShapeDtypeStruct((8, 192), F32)
    activations, input_grad, grad_b_query, grad_b_value = pl.pallas_call(
        hand_over,
        out_shape=(rows, rows, small, small),
        in_specs=[anywhere] * 3,
        out_specs=[in_hbm] * 4,
        scratch_shapes=[pltpu.SemaphoreType.DMA((4,))],
        compiler_params=pltpu.CompilerParams(vmem_limit_bytes=1024 * 1024),
    )(*results)
    return (
        activations.reshape(tokens.shape),
        input_grad.reshape(tokens.shape),
        grad_b_query,
        grad_b_value,
    )


def solution(mesh):
    batch = mesh.shape["batch"]
    in_specs = (
        P("batch", None),
        P("batch"),
        P(None, "head"),
        P(None, "head"),
        P(None, "head"),
        P("head", None),
        P(),
        P(),
        P(None, "head"),
        P(None, "head"),
        P(None, "head"),
        P("head", None),
        P(),
        P(),
        P("batch", None),
    )
    out_specs = (P("batch", None), P("batch", None), P(None, "head"), P(None, "head"))
    return jax.shard_map(
        functools.partial(body, batch),
        mesh=mesh,
        in_specs=in_specs,
        out_specs=out_specs,
        check_vma=False,
    )
```

```python
import functools

import jax
import jax.numpy as jnp
from jax import lax
from jax.experimental import pallas as pl
from jax.experimental.pallas import tpu as pltpu
from jax.sharding import PartitionSpec as P

HD = 64
BF16 = jnp.bfloat16
F32 = jnp.float32
MESH = pl.DeviceIdType.MESH

OUT, UP, DOWN, QKV, ADAPTER = 0, 1, 5, 9, 12
ITEMS = 12
OWN, SIB, FAR, FARSIB = 0, 1, 2, 3
OVER_Y = (16, 0, 0, 0, 0, 32, 32, 32, 32, 32, 32, 32)
TWICE = (1, 2, 3, 4)
GROUPS = ((0, 1), (1, 2), (3, 2), (5, 2), (7, 1), (8, 1), (9, 3))
SPANS = ((0, 128), (128, 256), (384, 384))
PIECES = (
    (0, 256, 0, 128),
    (0, 256, 128, 256),
    (0, 256, 384, 256),
    (0, 128, 640, 128),
    (128, 128, 640, 128),
)
SEND_GROUPS = ("y", "x", "z", "t", "d", "c", "w", "ctx", "dctx", "rows", "b", "l", "g")


def dot(left, right, left_dim=1, right_dim=0):
    return lax.dot_general(
        left, right, (((left_dim,), (right_dim,)), ((), ())), preferred_element_type=F32
    )


def norm(z):
    centre = z - jnp.mean(z, axis=-1, keepdims=True)
    inverse = lax.rsqrt(jnp.mean(centre * centre, axis=-1, keepdims=True) + 1e-05)
    return centre * inverse, inverse


def norm_back(scaled, normed, inverse):
    return inverse * (
        scaled
        - jnp.mean(scaled, axis=-1, keepdims=True)
        - normed * jnp.mean(scaled * normed, axis=-1, keepdims=True)
    )


def flip(index, bit):
    return index + bit - 2 * bit * ((index // bit) % 2)


def kernel(
    batch,
    lengths,
    tokens,
    w_query,
    w_key,
    w_value,
    w_out,
    w_up,
    w_down,
    down_query,
    down_value,
    up_query,
    up_value,
    gain_one,
    gain_two,
    cotangent,
    activations,
    input_grad,
    grads_out,
    x,
    w,
    raw_down,
    raw_up,
    gains,
    cot,
    adapter_up,
    ups_out,
    low,
    qkv,
    probs,
    log_sum,
    ctx_out,
    ctx_in,
    normed_one,
    inverse_one,
    hidden,
    hidden_low,
    act,
    slope,
    total,
    grad_z1,
    input_sum,
    dctx_out,
    dctx_in,
    grad_qkv,
    part_out,
    part_in,
    grads,
    grads_in,
    grads_all,
    grads_sums,
    local_sem,
    send_sem,
    recv_sem,
):
    b = lax.axis_index("batch")
    h = lax.axis_index("head")
    core = h % 2
    seq = h // 2
    far_seq = 1 - seq
    part = b % 4
    sibling = (b, flip(h, 1))
    across = (b, flip(h, 2))
    diagonal = (b, 3 - h)
    x_peer = (flip(b, 1), h)
    z_peer = (flip(b, 2), h)
    xz_peer = (flip(flip(b, 1), 2), h)
    batch_peers = [(flip(b, 1 << s), h) for s in range(2, batch.bit_length() - 1)]

    barrier = pltpu.get_barrier_semaphore()
    peers = [sibling, across, diagonal, x_peer, z_peer, xz_peer] + batch_peers
    for peer in peers:
        pl.semaphore_signal(barrier, inc=1, device_id=peer, device_id_type=MESH)

    recv_numbers = {}
    local_numbers = {}

    def copy(group, key, source, target, device):
        number = recv_numbers.setdefault(key, len(recv_numbers))
        return pltpu.make_async_remote_copy(
            src_ref=source,
            dst_ref=target,
            send_sem=send_sem.at[SEND_GROUPS.index(group)],
            recv_sem=recv_sem.at[number],
            device_id=device,
            device_id_type=MESH,
        )

    def send(group, key, source, target, device):
        copy(group, key, source, target, device).start()

    def arrived(key, target):
        copy("y", key, target, target, sibling).wait_recv()

    def sent(group, ref):
        copy(group, ("y", 0), ref, ref, sibling).wait_send()

    def local(key, source, target):
        number = local_numbers.setdefault(key, len(local_numbers))
        return pltpu.make_async_copy(source, target, local_sem.at[number])

    def load(key, source, target):
        local(key, source, target).start()

    def loaded(key, target):
        local(key, target, target).wait()

    for j, ref in enumerate((w_query, w_key, w_value)):
        load("qkv", ref, w.at[OWN, QKV + j])
    load("far", tokens.at[pl.ds(2 * far_seq, 2)], x.at[pl.ds(2 * far_seq, 2)])
    load("downs", down_query, raw_down.at[0])
    load("downs", down_value, raw_down.at[1])
    load("ups", up_query, raw_up.at[0])
    load("ups", up_value, raw_up.at[1])
    load("own", tokens.at[pl.ds(2 * seq, 2)], x.at[pl.ds(2 * seq, 2)])
    load("w", w_out, w.at[OWN, pl.ds(OUT, 1)])
    load("w", w_up, w.at[OWN, pl.ds(UP, 4)])
    load("w", w_down, w.at[OWN, pl.ds(DOWN, 4)])
    load("one", gain_one, gains.at[0])
    load("two", gain_two, gains.at[1])
    load("cot", cotangent.at[h], cot)

    far = w.at[FAR]
    px, pz, pd = flip(part, 1), flip(part, 2), 3 - part
    group_of = {}
    for first, count in GROUPS:
        for item in range(first, first + count):
            group_of[item] = first

    def rows_of(ref, item, index, start=0, count=48):
        return ref.at[item, pl.ds(pl.multiple_of(48 * index + start, 16), count)]

    def source_of(item):
        if item >= QKV:
            return w.at[OWN], item
        if item >= DOWN:
            return w_down, item - DOWN
        if item >= UP:
            return w_up, item - UP
        return w_out, item

    def send_part(*items):
        for item in items:
            source, at = source_of(item)
            mine, theirs = rows_of(source, at, part), rows_of(far, item, part)
            send("y", ("y", item), mine, theirs, across)

    def send_rest(*items):
        for item in items:
            source, at = source_of(item)
            count = OVER_Y[item]
            mine, theirs = rows_of(source, at, pd, 0, count), rows_of(far, item, pd, 0, count)
            send("t", ("f", group_of[item]), mine, theirs, across)

    def relay(*items):
        for item in items:
            mine = rows_of(far, item, part)
            arrived(("y", item), mine)
            twice = item in TWICE
            key = ("f", group_of[item])
            send("x", ("x", item) if twice else key, mine, mine, x_peer)
            send("z", ("z", item) if twice else key, mine, mine, z_peer)
            if not twice:
                count = OVER_Y[item]
                rest = rows_of(far, item, part, count, 48 - count)
                send("d", key, rest, rest, xz_peer)

    def relay_again(*items):
        for item in items:
            key = ("f", group_of[item])
            arrived(("x", item), rows_of(far, item, px))
            over_x = 32 if item % 2 else 16
            piece = rows_of(far, item, px, over_x, 48 - over_x)
            send("z", key, piece, piece, z_peer)
            arrived(("z", item), rows_of(far, item, pz))
            piece = rows_of(far, item, pz, 0, over_x)
            send("x", key, piece, piece, x_peer)

    def collect(group):
        first, count = GROUPS[group]
        items = pl.ds(first, count)
        arrived(("f", first), w.at[FAR, items, pl.ds(0, 48 if first in TWICE else 144)])
        if first < QKV:
            send("c", ("c", first), w.at[FAR, items], w.at[FARSIB, items], sibling)

    def collect_sibling(group):
        first, count = GROUPS[group]
        arrived(("c", first), w.at[FARSIB, pl.ds(first, count)])

    pl.semaphore_wait(barrier, len(peers))
    send_part(0)
    send_part(1)
    send_rest(0)
    send_part(2)
    send_part(3)
    send_part(4)
    send_part(5)
    send_part(6)
    pl.when(core == 1)(lambda: send_part(7))
    send("w", "so", w_out, w.at[SIB, pl.ds(OUT, 1)], sibling)
    send("w", "su", w_up, w.at[SIB, pl.ds(UP, 4)], sibling)
    send("w", "sd", w_down, w.at[SIB, pl.ds(DOWN, 4)], sibling)

    loaded("downs", raw_down)
    loaded("ups", raw_up)
    downs = jnp.concatenate([raw_down[0].astype(F32), raw_down[1].astype(F32)] * 2, axis=0)
    w[OWN, ADAPTER, :32] = downs.astype(BF16)
    w[FAR, ADAPTER, :32] = downs.astype(BF16)
    ups_out[0] = jnp.concatenate([raw_up[0].astype(F32), raw_up[1].astype(F32)], axis=0).astype(BF16)
    mine_up = lax.broadcasted_iota(jnp.int32, (16, 192), 0) < 8

    def spread_up(which):
        both = ups_out[which].astype(F32)
        adapter_up[which, :, :192] = jnp.where(mine_up, both, 0.0)
        adapter_up[which, :, 192:384] = jnp.zeros((16, 192), F32)
        adapter_up[which, :, 384:] = jnp.where(mine_up, 0.0, both)

    spread_up(0)

    def adapted(slot, count):
        return w[slot, QKV:].reshape(768, 768)[:count]

    def project(rows, which, slot, store):
        full = dot(adapted(slot, 592), x[pl.ds(2 * rows, 2)].reshape(512, 768), 1, 1)
        lows = full[576:].astype(BF16)
        ups = adapter_up[0 if slot == OWN else 1].astype(BF16)
        if store:
            low[...] = lows
        query = full[:192] + 2.0 * dot(ups[:, :192], lows, 0, 0)
        value = full[384:576] + 2.0 * dot(ups[:, 384:], lows, 0, 0)
        qkv[which, :192] = query.astype(BF16)
        qkv[which, 192:384] = full[192:384].astype(BF16)
        qkv[which, 384:] = value.astype(BF16)

    def head_rows(j, head):
        return slice(192 * j + HD * head, 192 * j + HD * (head + 1))

    def scores_of(rows, which, head):
        position = lax.broadcasted_iota(jnp.int32, (512, 1), 0)
        bias = jnp.where(position < lengths[rows], 0.0, -1e30)
        query = qkv[which, head_rows(0, head)] * jnp.asarray(0.125, BF16)
        return dot(qkv[which, head_rows(1, head)], query, 0, 0) + bias

    def attend(rows, which, context):
        for head in range(3):
            scores = scores_of(rows, which, head)
            top = jnp.max(scores, axis=0, keepdims=True)
            exponent = jnp.exp(scores - top)
            amount = jnp.sum(exponent, axis=0, keepdims=True)
            probs[which, head] = (exponent * (1.0 / amount)).astype(BF16)
            if which == 1:
                log_sum[0, head] = top + jnp.log(amount)
        for head in range(3):
            out = dot(qkv[which, head_rows(2, head)], probs[which, head]).astype(BF16)
            ctx_out[context, 0, head_rows(0, head)] = out[:, :256]
            ctx_out[context, 1, head_rows(0, head)] = out[:, 256:]

    loaded("qkv", w.at[OWN, pl.ds(QKV, 3)])
    loaded("far", x.at[pl.ds(2 * far_seq, 2)])
    project(far_seq, 1, OWN, False)
    attend(far_seq, 1, 1)
    send("ctx", "ctx", ctx_out.at[1, core], ctx_in.at[FAR], across)
    send("ctx", "ctx", ctx_out.at[1, 1 - core], ctx_in.at[FARSIB], diagonal)
    pl.when(core == 0)(lambda: send_part(7))
    send_part(8)
    send_rest(5)
    send_rest(6)
    send_rest(7)
    send_rest(8)
    send_part(9)
    send_part(10)
    send_part(11)
    send_rest(9)
    send_rest(10)
    send_rest(11)
    send("b", "b", ups_out.at[0], ups_out.at[1], across)
    send("l", "l", log_sum.at[0], log_sum.at[1], across)
    relay(0)
    loaded("own", x.at[pl.ds(2 * seq, 2)])
    project(seq, 0, OWN, True)
    relay(1)
    attend(seq, 0, 0)
    send("ctx", "ctx", ctx_out.at[0, 1 - core], ctx_in.at[SIB], sibling)
    ctx_in[OWN] = ctx_out[0, core]
    relay(2)
    relay(3)
    relay_again(1)
    relay(4)
    relay_again(2)
    relay(5)
    collect(0)
    relay_again(3)
    relay(6)
    relay_again(4)
    pl.when(core == 1)(lambda: relay(7))

    loaded("w", w.at[OWN, pl.ds(0, QKV)])
    loaded("one", gains.at[0])
    loaded("two", gains.at[1])
    loaded("cot", cot)
    arrived("so", w.at[SIB, pl.ds(OUT, 1)])
    collect_sibling(0)
    arrived("ctx", ctx_in.at[pl.ds(1, 3)])
    attn = dot(ctx_in[...].reshape(768, 256), w[:, OUT].reshape(768, 768), 0, 0)
    n1, r1 = norm(x[h].astype(F32) + attn)
    normed_one[...] = n1
    inverse_one[...] = r1
    h1 = n1 * gains[0:1]
    hidden[...] = h1
    hidden_low[...] = h1.astype(BF16)

    def go_up(slot):
        up = dot(hidden_low[...], w[slot, UP : UP + 4].reshape(768, 768))
        phi = 0.5 * (1.0 + lax.erf(up * 0.7071067811865476))
        slope[slot] = phi + up * (0.3989422804014327 * jnp.exp(-0.5 * up * up))
        act[slot] = (up * phi).astype(BF16)

    def go_down(slot, first=0, count=4):
        rows = slice(192 * first, 192 * (first + count))
        weights = w[slot, DOWN + first : DOWN + first + count].reshape(192 * count, 768)
        return dot(act[slot, :, rows], weights)

    pl.when(core == 1)(lambda: relay(8))
    go_up(OWN)
    pl.when(core == 0)(lambda: relay(7))
    arrived("su", w.at[SIB, pl.ds(UP, 4)])
    go_up(SIB)
    arrived("sd", w.at[SIB, pl.ds(DOWN, 4)])
    total[...] = hidden[...] + go_down(OWN) + go_down(SIB)
    pl.when(core == 0)(lambda: relay(8))
    collect(1)
    collect(2)
    go_up(FAR)
    collect_sibling(1)
    collect_sibling(2)
    go_up(FARSIB)
    collect(3)
    collect(4)
    collect(5)
    total[...] += go_down(FAR, 0, 3)
    collect_sibling(3)
    collect_sibling(4)
    total[...] += go_down(FARSIB, 0, 3)
    total[...] += go_down(FAR, 3, 1)
    relay(9)
    collect_sibling(5)
    z2 = total[...] + go_down(FARSIB, 3, 1)

    n2, r2 = norm(z2)
    position = lax.broadcasted_iota(jnp.int32, (256, 1), 0) + 256 * core
    valid = (position < lengths[seq]).astype(F32)
    activations[h] = (valid * (n2 * gains[1:2])).astype(BF16)
    send("rows", "ay", activations.at[h], activations.at[h], across)
    send("rows", "all", activations.at[h], activations.at[h], sibling)
    d_z2 = norm_back(cot[...].astype(F32) * valid * gains[1:2], n2, r2)
    d_z2_low = d_z2.astype(BF16)
    relay(10)

    steps = []
    for slot in range(4):
        d_act = dot(d_z2_low, w[slot, DOWN : DOWN + 4].reshape(768, 768), 1, 1)
        steps.append((d_act * slope[slot]).astype(BF16))
    grad_h1 = d_z2
    for slot in range(4):
        grad_h1 = grad_h1 + dot(steps[slot], w[slot, UP : UP + 4].reshape(768, 768), 1, 1)

    d_z1 = norm_back(grad_h1 * gains[0:1], normed_one[...], inverse_one[...])
    grad_z1[...] = d_z1
    d_z1_low = d_z1.astype(BF16)
    relay(11)

    def d_context(first):
        pair = [w[first, OUT], w[first + 2, OUT]]
        d_ctx = dot(jnp.concatenate(pair, axis=0), d_z1_low, 1, 1).astype(BF16)
        dctx_out[first] = d_ctx[:192]
        dctx_out[first + 2] = d_ctx[192:]

    d_context(SIB)
    send("dctx", "dctx", dctx_out.at[SIB], dctx_in.at[core, 0], sibling)
    send("dctx", "dctx", dctx_out.at[FARSIB], dctx_in.at[core, 1], sibling)
    d_context(OWN)
    dctx_in[core, 0] = dctx_out[OWN]
    dctx_in[core, 1] = dctx_out[FAR]
    arrived("dctx", dctx_in.at[1 - core])

    def attend_back(which):
        d_scores = []
        for head in range(3):
            rows = head_rows(0, head)
            d_out = jnp.concatenate([dctx_in[0, which, rows], dctx_in[1, which, rows]], axis=1)
            if which == 0:
                probability = probs[0, head].astype(F32)
            else:
                probability = jnp.exp(scores_of(seq, 1, head) - log_sum[1, head])
                probs[1, head] = probability.astype(BF16)
            d_weights = dot(qkv[which, head_rows(2, head)], d_out, 0, 0)
            if which == 0:
                context = jnp.concatenate([ctx_out[0, 0, rows], ctx_out[0, 1, rows]], axis=1)
                products = d_out.astype(F32) * context.astype(F32)
            else:
                products = probability * d_weights
            mean = jnp.sum(products, axis=0, keepdims=True)
            d_scores.append((probability * (d_weights - mean)).astype(BF16))
        for head in range(3):
            rows = head_rows(0, head)
            d_out = jnp.concatenate([dctx_in[0, which, rows], dctx_in[1, which, rows]], axis=1)
            d_query = dot(qkv[which, head_rows(1, head)] * jnp.asarray(0.125, BF16), d_scores[head]).astype(BF16)
            d_key = dot(d_scores[head], qkv[which, head_rows(0, head)] * jnp.asarray(0.125, BF16), 1, 1)
            d_value = dot(probs[which, head], d_out, 1, 1)
            pieces = (d_query, d_key.astype(BF16).T, d_value.astype(BF16).T)
            for j, piece in enumerate(pieces):
                grad_qkv[which, head_rows(j, head)] = piece

    def adapter_grads(which):
        for j in range(2):
            rows = slice(384 * j, 384 * j + 192)
            both = dot(low[...], grad_qkv[which, rows], 1, 1)
            grads[which, j] = 2.0 * both[8 * j : 8 * j + 8]

    def adapter_rows(which):
        d_low = 2.0 * dot(adapter_up[which].astype(BF16), grad_qkv[which, :576])
        coarse = d_low.astype(BF16)
        fine = (d_low - coarse.astype(F32)).astype(BF16)
        grad_qkv[which, 576:] = jnp.concatenate([coarse, fine], axis=0)

    def input_part(which, columns, half=None):
        weights = w[OWN if which == 0 else FAR, QKV:].reshape(768, 768)[:608, columns]
        if half is None:
            return dot(grad_qkv[which], weights, 0, 0).reshape(2, 256, 768)
        rows = pl.ds(pl.multiple_of(256 * half, 256), 256)
        return dot(grad_qkv[which, :, rows], weights, 0, 0)

    attend_back(0)
    adapter_rows(0)
    input_sum[...] = input_part(0, slice(0, 768))
    input_sum[core] += grad_z1[...]
    adapter_grads(0)

    collect(6)
    arrived("b", ups_out.at[1])
    spread_up(1)
    arrived("l", log_sum.at[1])
    project(seq, 1, FAR, False)
    attend_back(1)
    adapter_rows(1)
    spans = [(t, slice(first, first + count)) for t, (first, count) in enumerate(SPANS)]
    def piece_of(rows, n):
        row, count, column, width = PIECES[n]
        return input_grad.at[rows, pl.ds(row, count), pl.ds(column, width)]

    def give(t):
        columns = spans[t][1]
        given = input_sum[1 - core, :, columns] + input_part(1, columns, 1 - core)
        part_out[:, columns] = given.astype(BF16)
        send("rows", ("p", t), part_out.at[:, columns], part_in.at[:, columns], sibling)

    def take(t):
        columns = spans[t][1]
        own = input_sum[core, :, columns] + input_part(1, columns, core)
        arrived(("p", t), part_in.at[:, columns])
        input_grad[h, :, columns] = (own + part_in[:, columns].astype(F32)).astype(BF16)
        for n, (row, rows, column, width) in enumerate(PIECES):
            if columns.start <= column < columns.stop:
                block = piece_of(h, n)
                send("rows", ("i", n), block, block, across)
                if n == len(PIECES) - 1:
                    send("rows", "all", block, block, diagonal)

    give(0)
    adapter_grads(1)
    send("g", "g", grads.at[1], grads_in, across)
    give(1)
    take(0)
    give(2)
    take(1)
    take(2)
    send("rows", "all", input_grad.at[h], input_grad.at[h], sibling)

    def pass_on(n):
        block = piece_of(flip(h, 2), n)
        arrived(("i", n), block)
        if n < len(PIECES) - 1:
            send("rows", "all", block, block, sibling)

    arrived("ay", activations.at[flip(h, 2)])
    send("rows", "all", activations.at[flip(h, 2)], activations.at[flip(h, 2)], sibling)
    arrived("g", grads_in)
    grads_all[part] = grads[0] + grads_in[...]
    for peer in (x_peer, z_peer, xz_peer):
        send("g", "sums", grads_all.at[part], grads_all.at[part], peer)
    pass_on(0)
    arrived("sums", grads_all.at[pl.ds(0, 3)])
    sums = (grads_all[0] + grads_all[1]) + (grads_all[2] + grads_all[3])
    for n, peer in enumerate(batch_peers):
        grads_sums[2 * n] = sums
        send("g", ("g", n), grads_sums.at[2 * n], grads_sums.at[2 * n + 1], peer)
        if n == 0:
            for m in range(1, len(PIECES)):
                pass_on(m)
        arrived(("g", n), grads_sums.at[2 * n + 1])
        sums = sums + grads_sums[2 * n + 1]
    grads_out[...] = sums
    for n in range(1, 1 if batch_peers else len(PIECES)):
        pass_on(n)
    arrived("all", activations)

    def rows_block(count):
        tiles = count // 16
        shapes = [(m, n, tiles // (m * n)) for m in (1, 2, 3, 4) for n in range(1, 13) if tiles % (m * n) == 0]
        inner, outer, depth = next(shape for shape in shapes if shape[2] <= 12)
        return w.at[pl.ds(0, inner), pl.ds(0, outer), pl.ds(0, 16 * depth)]

    sent("y", w.at[FAR, pl.ds(0, 3)])
    sent("x", rows_block(48 * ITEMS + 24 * len(TWICE)))
    sent("z", rows_block(48 * ITEMS + 24 * len(TWICE)))
    sent("t", rows_block(sum(OVER_Y)))
    sent("d", rows_block(sum(48 - OVER_Y[n] for n in range(ITEMS) if n not in TWICE)))
    sent("c", w.at[FAR, pl.ds(0, 9)])
    sent("w", w.at[SIB, pl.ds(0, 9)])
    sent("ctx", ctx_in.at[pl.ds(0, 3)])
    sent("dctx", dctx_in.at[0])
    sent("rows", w.at[pl.ds(0, 4), pl.ds(0, 7), pl.ds(0, 64)])
    sent("b", ups_out.at[0])
    sent("l", log_sum.at[0])
    sent("g", grads_sums.at[pl.ds(0, 4 + len(batch_peers))])


def hand_over(activations, input_grad, grads, *rest):
    targets, sem = rest[:4], rest[4]
    sources = (activations, input_grad, grads.at[0], grads.at[1])
    copies = [
        pltpu.make_async_copy(source, target, sem.at[n])
        for n, (source, target) in enumerate(zip(sources, targets))
    ]
    for c in copies:
        c.start()
    for c in copies:
        c.wait()


def body(batch, *given):
    (
        tokens,
        lengths,
        w_query,
        w_key,
        w_value,
        w_out,
        down_query,
        down_value,
        up_query,
        up_value,
        w_up,
        w_down,
        gain_attn,
        gain_ffn,
        cotangent,
    ) = given
    anywhere = pl.BlockSpec(memory_space=pl.ANY)
    in_vmem = pl.BlockSpec(memory_space=pltpu.VMEM)
    in_hbm = pl.BlockSpec(memory_space=pltpu.HBM)
    vmem = pltpu.VMEM
    results = pl.pallas_call(
        functools.partial(kernel, batch),
        out_shape=(
            vmem((4, 256, 768), BF16),
            vmem((4, 256, 768), BF16),
            vmem((2, 8, 192), F32),
        ),
        in_specs=[pl.BlockSpec(memory_space=pltpu.SMEM)] + [in_hbm] * 14,
        out_specs=(in_vmem,) * 3,
        scratch_shapes=[
            vmem((4, 256, 768), BF16),
            vmem((4, 13, 192, 768), BF16),
            vmem((2, 8, 768), BF16),
            vmem((2, 8, 192), BF16),
            vmem((2, 768), F32),
            vmem((256, 768), BF16),
            vmem((2, 16, 576), F32),
            vmem((2, 16, 192), BF16),
            vmem((16, 512), BF16),
            vmem((2, 576, 512), BF16),
            vmem((2, 3, 512, 512), BF16),
            vmem((2, 3, 1, 512), F32),
            vmem((2, 2, 192, 256), BF16),
            vmem((4, 192, 256), BF16),
            vmem((256, 768), F32),
            vmem((256, 1), F32),
            vmem((256, 768), F32),
            vmem((256, 768), BF16),
            vmem((4, 256, 768), BF16),
            vmem((4, 256, 768), F32),
            vmem((256, 768), F32),
            vmem((256, 768), F32),
            vmem((2, 256, 768), F32),
            vmem((4, 192, 256), BF16),
            vmem((2, 2, 192, 256), BF16),
            vmem((2, 608, 512), BF16),
            vmem((256, 768), BF16),
            vmem((256, 768), BF16),
            vmem((2, 2, 8, 192), F32),
            vmem((2, 8, 192), F32),
            vmem((4, 2, 8, 192), F32),
            vmem((2 * batch.bit_length(), 2, 8, 192), F32),
            pltpu.SemaphoreType.DMA((9,)),
            pltpu.SemaphoreType.DMA((len(SEND_GROUPS),)),
            pltpu.SemaphoreType.DMA((33 + 2 * len(TWICE) + batch.bit_length() + len(SPANS) + len(PIECES),)),
        ],
        compiler_params=pltpu.CompilerParams(
            collective_id=0, has_side_effects=True, vmem_limit_bytes=56 * 1024 * 1024
        ),
        cost_estimate=pl.CostEstimate(
            flops=11_000_000_000, bytes_accessed=20_000_000, transcendentals=4_000_000
        ),
    )(
        lengths,
        tokens.reshape(4, 256, 768),
        w_query.T,
        w_key.T,
        w_value.T,
        w_out.reshape(1, 192, 768),
        w_up.reshape(4, 192, 768),
        w_down.reshape(4, 192, 768),
        down_query.T,
        down_value.T,
        up_query,
        up_value,
        gain_attn,
        gain_ffn,
        cotangent.reshape(4, 256, 768),
    )
    rows = jax.ShapeDtypeStruct((4, 256, 768), BF16)
    small = jax.ShapeDtypeStruct((8, 192), F32)
    activations, input_grad, grad_b_query, grad_b_value = pl.pallas_call(
        hand_over,
        out_shape=(rows, rows, small, small),
        in_specs=[anywhere] * 3,
        out_specs=[in_hbm] * 4,
        scratch_shapes=[pltpu.SemaphoreType.DMA((4,))],
        compiler_params=pltpu.CompilerParams(vmem_limit_bytes=1024 * 1024),
    )(*results)
    return (
        activations.reshape(tokens.shape),
        input_grad.reshape(tokens.shape),
        grad_b_query,
        grad_b_value,
    )


def solution(mesh):
    batch = mesh.shape["batch"]
    in_specs = (
        P("batch", None),
        P("batch"),
        P(None, "head"),
        P(None, "head"),
        P(None, "head"),
        P("head", None),
        P(),
        P(),
        P(None, "head"),
        P(None, "head"),
        P(None, "head"),
        P("head", None),
        P(),
        P(),
        P("batch", None),
    )
    out_specs = (P("batch", None), P("batch", None), P(None, "head"), P(None, "head"))
    return jax.shard_map(
        functools.partial(body, batch),
        mesh=mesh,
        in_specs=in_specs,
        out_specs=out_specs,
        check_vma=False,
    )
```

```python
import functools

import jax
import jax.numpy as jnp
from jax import lax
from jax.experimental import pallas as pl
from jax.experimental.pallas import tpu as pltpu
from jax.sharding import PartitionSpec as P

HD = 64
BF16 = jnp.bfloat16
F32 = jnp.float32
MESH = pl.DeviceIdType.MESH

OUT, UP, DOWN, QKV, ADAPTER = 0, 1, 5, 9, 12
ITEMS = 12
OWN, SIB, FAR, FARSIB = 0, 1, 2, 3
OVER_Y = (16, 0, 0, 0, 0, 32, 32, 32, 32, 32, 32, 32)
TWICE = (1, 2, 3, 4)
GROUPS = ((0, 1), (1, 2), (3, 2), (5, 2), (7, 1), (8, 1), (9, 3))
SPANS = ((0, 128), (128, 256), (384, 384))
PIECES = (
    (0, 256, 0, 128),
    (0, 256, 128, 256),
    (0, 256, 384, 256),
    (0, 128, 640, 128),
    (128, 128, 640, 128),
)
SEND_GROUPS = ("y", "x", "z", "t", "d", "c", "w", "ctx", "dctx", "rows", "b", "l", "g")


def dot(left, right, left_dim=1, right_dim=0):
    return lax.dot_general(
        left, right, (((left_dim,), (right_dim,)), ((), ())), preferred_element_type=F32
    )


def norm(z):
    centre = z - jnp.mean(z, axis=-1, keepdims=True)
    inverse = lax.rsqrt(jnp.mean(centre * centre, axis=-1, keepdims=True) + 1e-05)
    return centre * inverse, inverse


def norm_back(scaled, normed, inverse):
    return inverse * (
        scaled
        - jnp.mean(scaled, axis=-1, keepdims=True)
        - normed * jnp.mean(scaled * normed, axis=-1, keepdims=True)
    )


def flip(index, bit):
    return index + bit - 2 * bit * ((index // bit) % 2)


def kernel(
    batch,
    lengths,
    tokens,
    w_query,
    w_key,
    w_value,
    w_out,
    w_up,
    w_down,
    down_query,
    down_value,
    up_query,
    up_value,
    gain_one,
    gain_two,
    cotangent,
    activations,
    input_grad,
    grads_out,
    x,
    w,
    raw_down,
    raw_up,
    gains,
    cot,
    adapter_up,
    ups_out,
    low,
    qkv,
    probs,
    log_sum,
    ctx_out,
    ctx_in,
    normed_one,
    inverse_one,
    hidden,
    hidden_low,
    act,
    slope,
    total,
    grad_z1,
    input_sum,
    dctx_out,
    dctx_in,
    grad_qkv,
    part_out,
    part_in,
    grads,
    grads_in,
    grads_all,
    grads_sums,
    local_sem,
    send_sem,
    recv_sem,
):
    b = lax.axis_index("batch")
    h = lax.axis_index("head")
    core = h % 2
    seq = h // 2
    far_seq = 1 - seq
    part = b % 4
    sibling = (b, flip(h, 1))
    across = (b, flip(h, 2))
    diagonal = (b, 3 - h)
    x_peer = (flip(b, 1), h)
    z_peer = (flip(b, 2), h)
    xz_peer = (flip(flip(b, 1), 2), h)
    batch_peers = [(flip(b, 1 << s), h) for s in range(2, batch.bit_length() - 1)]

    barrier = pltpu.get_barrier_semaphore()
    peers = [sibling, across, diagonal, x_peer, z_peer, xz_peer] + batch_peers
    for peer in peers:
        pl.semaphore_signal(barrier, inc=1, device_id=peer, device_id_type=MESH)

    recv_numbers = {}
    local_numbers = {}

    def copy(group, key, source, target, device):
        number = recv_numbers.setdefault(key, len(recv_numbers))
        return pltpu.make_async_remote_copy(
            src_ref=source,
            dst_ref=target,
            send_sem=send_sem.at[SEND_GROUPS.index(group)],
            recv_sem=recv_sem.at[number],
            device_id=device,
            device_id_type=MESH,
        )

    def send(group, key, source, target, device):
        copy(group, key, source, target, device).start()

    def arrived(key, target):
        copy("y", key, target, target, sibling).wait_recv()

    def sent(group, ref):
        copy(group, ("y", 0), ref, ref, sibling).wait_send()

    def local(key, source, target):
        number = local_numbers.setdefault(key, len(local_numbers))
        return pltpu.make_async_copy(source, target, local_sem.at[number])

    def load(key, source, target):
        local(key, source, target).start()

    def loaded(key, target):
        local(key, target, target).wait()

    for j, ref in enumerate((w_query, w_key, w_value)):
        load("qkv", ref, w.at[OWN, QKV + j])
    load("far", tokens.at[pl.ds(2 * far_seq, 2)], x.at[pl.ds(2 * far_seq, 2)])
    load("downs", down_query, raw_down.at[0])
    load("downs", down_value, raw_down.at[1])
    load("ups", up_query, raw_up.at[0])
    load("ups", up_value, raw_up.at[1])
    load("own", tokens.at[pl.ds(2 * seq, 2)], x.at[pl.ds(2 * seq, 2)])
    load("w", w_out, w.at[OWN, pl.ds(OUT, 1)])
    load("w", w_up, w.at[OWN, pl.ds(UP, 4)])
    load("w", w_down, w.at[OWN, pl.ds(DOWN, 4)])
    load("one", gain_one, gains.at[0])
    load("two", gain_two, gains.at[1])
    load("cot", cotangent.at[h], cot)

    far = w.at[FAR]
    px, pz, pd = flip(part, 1), flip(part, 2), 3 - part
    group_of = {}
    for first, count in GROUPS:
        for item in range(first, first + count):
            group_of[item] = first

    def rows_of(ref, item, index, start=0, count=48):
        return ref.at[item, pl.ds(pl.multiple_of(48 * index + start, 16), count)]

    def source_of(item):
        if item >= QKV:
            return w.at[OWN], item
        if item >= DOWN:
            return w_down, item - DOWN
        if item >= UP:
            return w_up, item - UP
        return w_out, item

    def send_part(*items):
        for item in items:
            source, at = source_of(item)
            mine, theirs = rows_of(source, at, part), rows_of(far, item, part)
            send("y", ("y", item), mine, theirs, across)

    def send_rest(*items):
        for item in items:
            source, at = source_of(item)
            count = OVER_Y[item]
            mine, theirs = rows_of(source, at, pd, 0, count), rows_of(far, item, pd, 0, count)
            send("t", ("f", group_of[item]), mine, theirs, across)

    def relay(*items):
        for item in items:
            mine = rows_of(far, item, part)
            arrived(("y", item), mine)
            twice = item in TWICE
            key = ("f", group_of[item])
            send("x", ("x", item) if twice else key, mine, mine, x_peer)
            send("z", ("z", item) if twice else key, mine, mine, z_peer)
            if not twice:
                count = OVER_Y[item]
                rest = rows_of(far, item, part, count, 48 - count)
                send("d", key, rest, rest, xz_peer)

    def relay_again(*items):
        for item in items:
            key = ("f", group_of[item])
            arrived(("x", item), rows_of(far, item, px))
            over_x = 32 if item % 2 else 16
            piece = rows_of(far, item, px, over_x, 48 - over_x)
            send("z", key, piece, piece, z_peer)
            arrived(("z", item), rows_of(far, item, pz))
            piece = rows_of(far, item, pz, 0, over_x)
            send("x", key, piece, piece, x_peer)

    def collect(group):
        first, count = GROUPS[group]
        items = pl.ds(first, count)
        arrived(("f", first), w.at[FAR, items, pl.ds(0, 48 if first in TWICE else 144)])
        if first < QKV:
            send("c", ("c", first), w.at[FAR, items], w.at[FARSIB, items], sibling)

    def collect_sibling(group):
        first, count = GROUPS[group]
        arrived(("c", first), w.at[FARSIB, pl.ds(first, count)])

    pl.semaphore_wait(barrier, len(peers))
    send_part(0)
    send_part(1)
    send_rest(0)
    send_part(2)
    send_part(3)
    send_part(4)
    send_part(5)
    send_part(6)
    pl.when(core == 1)(lambda: send_part(7))
    send("w", "so", w_out, w.at[SIB, pl.ds(OUT, 1)], sibling)
    send("w", "su", w_up, w.at[SIB, pl.ds(UP, 4)], sibling)
    send("w", "sd", w_down, w.at[SIB, pl.ds(DOWN, 4)], sibling)

    loaded("downs", raw_down)
    loaded("ups", raw_up)
    downs = jnp.concatenate([raw_down[0].astype(F32), raw_down[1].astype(F32)] * 2, axis=0)
    w[OWN, ADAPTER, :32] = downs.astype(BF16)
    w[FAR, ADAPTER, :32] = downs.astype(BF16)
    ups_out[0] = jnp.concatenate([raw_up[0].astype(F32), raw_up[1].astype(F32)], axis=0).astype(BF16)
    mine_up = lax.broadcasted_iota(jnp.int32, (16, 192), 0) < 8

    def spread_up(which):
        both = ups_out[which].astype(F32)
        adapter_up[which, :, :192] = jnp.where(mine_up, both, 0.0)
        adapter_up[which, :, 192:384] = jnp.zeros((16, 192), F32)
        adapter_up[which, :, 384:] = jnp.where(mine_up, 0.0, both)

    spread_up(0)

    def adapted(slot, count):
        return w[slot, QKV:].reshape(768, 768)[:count]

    def project(rows, which, slot, store):
        full = dot(adapted(slot, 592), x[pl.ds(2 * rows, 2)].reshape(512, 768), 1, 1)
        lows = full[576:].astype(BF16)
        ups = adapter_up[0 if slot == OWN else 1].astype(BF16)
        if store:
            low[...] = lows
        query = full[:192] + 2.0 * dot(ups[:, :192], lows, 0, 0)
        value = full[384:576] + 2.0 * dot(ups[:, 384:], lows, 0, 0)
        qkv[which, :192] = query.astype(BF16)
        qkv[which, 192:384] = full[192:384].astype(BF16)
        qkv[which, 384:] = value.astype(BF16)

    def head_rows(j, head):
        return slice(192 * j + HD * head, 192 * j + HD * (head + 1))

    def scores_of(rows, which, head):
        position = lax.broadcasted_iota(jnp.int32, (512, 1), 0)
        bias = jnp.where(position < lengths[rows], 0.0, -1e30)
        query = qkv[which, head_rows(0, head)] * jnp.asarray(0.125, BF16)
        return dot(qkv[which, head_rows(1, head)], query, 0, 0) + bias

    def attend(rows, which, context):
        for head in range(3):
            scores = scores_of(rows, which, head)
            top = jnp.max(scores, axis=0, keepdims=True)
            exponent = jnp.exp(scores - top)
            amount = jnp.sum(exponent, axis=0, keepdims=True)
            probs[which, head] = (exponent * (1.0 / amount)).astype(BF16)
            if which == 1:
                log_sum[0, head] = top + jnp.log(amount)
        for head in range(3):
            out = dot(qkv[which, head_rows(2, head)], probs[which, head]).astype(BF16)
            ctx_out[context, 0, head_rows(0, head)] = out[:, :256]
            ctx_out[context, 1, head_rows(0, head)] = out[:, 256:]

    loaded("qkv", w.at[OWN, pl.ds(QKV, 3)])
    loaded("far", x.at[pl.ds(2 * far_seq, 2)])
    project(far_seq, 1, OWN, False)
    attend(far_seq, 1, 1)
    send("ctx", "ctx", ctx_out.at[1, core], ctx_in.at[FAR], across)
    send("ctx", "ctx", ctx_out.at[1, 1 - core], ctx_in.at[FARSIB], diagonal)
    pl.when(core == 0)(lambda: send_part(7))
    send_part(8)
    send_rest(5)
    send_rest(6)
    send_rest(7)
    send_rest(8)
    send_part(9)
    send_part(10)
    send_part(11)
    send_rest(9)
    send_rest(10)
    send_rest(11)
    send("b", "b", ups_out.at[0], ups_out.at[1], across)
    send("l", "l", log_sum.at[0], log_sum.at[1], across)
    relay(0)
    loaded("own", x.at[pl.ds(2 * seq, 2)])
    project(seq, 0, OWN, True)
    relay(1)
    attend(seq, 0, 0)
    send("ctx", "ctx", ctx_out.at[0, 1 - core], ctx_in.at[SIB], sibling)
    ctx_in[OWN] = ctx_out[0, core]
    relay(2)
    relay(3)
    relay_again(1)
    relay(4)
    relay_again(2)
    relay(5)
    collect(0)
    relay_again(3)
    relay(6)
    relay_again(4)
    pl.when(core == 1)(lambda: relay(7))

    loaded("w", w.at[OWN, pl.ds(0, QKV)])
    loaded("one", gains.at[0])
    loaded("two", gains.at[1])
    loaded("cot", cot)
    arrived("so", w.at[SIB, pl.ds(OUT, 1)])
    collect_sibling(0)
    arrived("ctx", ctx_in.at[pl.ds(1, 3)])
    attn = dot(ctx_in[...].reshape(768, 256), w[:, OUT].reshape(768, 768), 0, 0)
    n1, r1 = norm(x[h].astype(F32) + attn)
    normed_one[...] = n1
    inverse_one[...] = r1
    h1 = n1 * gains[0:1]
    hidden[...] = h1
    hidden_low[...] = h1.astype(BF16)

    def go_up(slot):
        up = dot(hidden_low[...], w[slot, UP : UP + 4].reshape(768, 768))
        phi = 0.5 * (1.0 + lax.erf(up * 0.7071067811865476))
        slope[slot] = phi + up * (0.3989422804014327 * jnp.exp(-0.5 * up * up))
        act[slot] = (up * phi).astype(BF16)

    def go_down(slot, first=0, count=4):
        rows = slice(192 * first, 192 * (first + count))
        weights = w[slot, DOWN + first : DOWN + first + count].reshape(192 * count, 768)
        return dot(act[slot, :, rows], weights)

    pl.when(core == 1)(lambda: relay(8))
    go_up(OWN)
    pl.when(core == 0)(lambda: relay(7))
    arrived("su", w.at[SIB, pl.ds(UP, 4)])
    go_up(SIB)
    arrived("sd", w.at[SIB, pl.ds(DOWN, 4)])
    total[...] = hidden[...] + go_down(OWN) + go_down(SIB)
    pl.when(core == 0)(lambda: relay(8))
    collect(1)
    collect(2)
    go_up(FAR)
    collect_sibling(1)
    collect_sibling(2)
    go_up(FARSIB)
    collect(3)
    collect(4)
    collect(5)
    total[...] += go_down(FAR, 0, 3)
    collect_sibling(3)
    collect_sibling(4)
    total[...] += go_down(FARSIB, 0, 3)
    total[...] += go_down(FAR, 3, 1)
    relay(9)
    collect_sibling(5)
    z2 = total[...] + go_down(FARSIB, 3, 1)

    n2, r2 = norm(z2)
    position = lax.broadcasted_iota(jnp.int32, (256, 1), 0) + 256 * core
    valid = (position < lengths[seq]).astype(F32)
    activations[h] = (valid * (n2 * gains[1:2])).astype(BF16)
    send("rows", "ay", activations.at[h], activations.at[h], across)
    send("rows", "all", activations.at[h], activations.at[h], sibling)
    d_z2 = norm_back(cot[...].astype(F32) * valid * gains[1:2], n2, r2)
    d_z2_low = d_z2.astype(BF16)
    relay(10)

    steps = []
    for slot in range(4):
        d_act = dot(d_z2_low, w[slot, DOWN : DOWN + 4].reshape(768, 768), 1, 1)
        steps.append((d_act * slope[slot]).astype(BF16))
    grad_h1 = d_z2
    for slot in range(4):
        grad_h1 = grad_h1 + dot(steps[slot], w[slot, UP : UP + 4].reshape(768, 768), 1, 1)

    d_z1 = norm_back(grad_h1 * gains[0:1], normed_one[...], inverse_one[...])
    grad_z1[...] = d_z1
    d_z1_low = d_z1.astype(BF16)
    relay(11)

    dctx_out[SIB] = dot(w[SIB, OUT], d_z1_low, 1, 1).astype(BF16)
    send("dctx", "dctx", dctx_out.at[SIB], dctx_in.at[core, 0], sibling)
    rest = jnp.concatenate([w[FARSIB, OUT], w[OWN, OUT], w[FAR, OUT]], axis=0)
    d_ctx = dot(rest, d_z1_low, 1, 1).astype(BF16)
    dctx_out[FARSIB] = d_ctx[:192]
    send("dctx", "far dctx", dctx_out.at[FARSIB], dctx_in.at[core, 1], sibling)
    dctx_out[OWN] = d_ctx[192:384]
    dctx_out[FAR] = d_ctx[384:]
    dctx_in[core, 0] = dctx_out[OWN]
    dctx_in[core, 1] = dctx_out[FAR]
    arrived("dctx", dctx_in.at[1 - core, 0])

    def attend_back(which):
        d_scores = []
        for head in range(3):
            rows = head_rows(0, head)
            d_out = jnp.concatenate([dctx_in[0, which, rows], dctx_in[1, which, rows]], axis=1)
            if which == 0:
                probability = probs[0, head].astype(F32)
            else:
                probability = jnp.exp(scores_of(seq, 1, head) - log_sum[1, head])
                probs[1, head] = probability.astype(BF16)
            d_weights = dot(qkv[which, head_rows(2, head)], d_out, 0, 0)
            mean = jnp.sum(probability * d_weights, axis=0, keepdims=True)
            d_scores.append((probability * (d_weights - mean)).astype(BF16))
        for head in range(3):
            rows = head_rows(0, head)
            d_out = jnp.concatenate([dctx_in[0, which, rows], dctx_in[1, which, rows]], axis=1)
            d_query = (0.125 * dot(qkv[which, head_rows(1, head)], d_scores[head])).astype(BF16)
            d_key = 0.125 * dot(d_scores[head], qkv[which, head_rows(0, head)], 1, 1)
            d_value = dot(probs[which, head], d_out, 1, 1)
            pieces = (d_query, d_key.astype(BF16).T, d_value.astype(BF16).T)
            for j, piece in enumerate(pieces):
                grad_qkv[which, head_rows(j, head)] = piece

    def adapter_grads(which):
        for j in range(2):
            rows = slice(384 * j, 384 * j + 192)
            both = dot(low[...], grad_qkv[which, rows], 1, 1)
            grads[which, j] = 2.0 * both[8 * j : 8 * j + 8]

    def adapter_rows(which):
        d_low = 2.0 * dot(adapter_up[which].astype(BF16), grad_qkv[which, :576])
        coarse = d_low.astype(BF16)
        fine = (d_low - coarse.astype(F32)).astype(BF16)
        grad_qkv[which, 576:] = jnp.concatenate([coarse, fine], axis=0)

    def input_part(which, columns, half=None):
        weights = w[OWN if which == 0 else FAR, QKV:].reshape(768, 768)[:608, columns]
        if half is None:
            return dot(grad_qkv[which], weights, 0, 0).reshape(2, 256, 768)
        rows = pl.ds(pl.multiple_of(256 * half, 256), 256)
        return dot(grad_qkv[which, :, rows], weights, 0, 0)

    attend_back(0)
    adapter_rows(0)
    input_sum[...] = input_part(0, slice(0, 768))
    input_sum[core] += grad_z1[...]
    adapter_grads(0)

    collect(6)
    arrived("b", ups_out.at[1])
    spread_up(1)
    arrived("l", log_sum.at[1])
    arrived("far dctx", dctx_in.at[1 - core, 1])
    project(seq, 1, FAR, False)
    attend_back(1)
    adapter_rows(1)
    spans = [(t, slice(first, first + count)) for t, (first, count) in enumerate(SPANS)]
    def piece_of(rows, n):
        row, count, column, width = PIECES[n]
        return input_grad.at[rows, pl.ds(row, count), pl.ds(column, width)]

    def give(t):
        columns = spans[t][1]
        given = input_sum[1 - core, :, columns] + input_part(1, columns, 1 - core)
        part_out[:, columns] = given.astype(BF16)
        send("rows", ("p", t), part_out.at[:, columns], part_in.at[:, columns], sibling)

    def take(t):
        columns = spans[t][1]
        own = input_sum[core, :, columns] + input_part(1, columns, core)
        arrived(("p", t), part_in.at[:, columns])
        input_grad[h, :, columns] = (own + part_in[:, columns].astype(F32)).astype(BF16)
        for n, (row, rows, column, width) in enumerate(PIECES):
            if columns.start <= column < columns.stop:
                block = piece_of(h, n)
                send("rows", ("i", n), block, block, across)
                if n == len(PIECES) - 1:
                    send("rows", "all", block, block, diagonal)

    give(0)
    adapter_grads(1)
    send("g", "g", grads.at[1], grads_in, across)
    give(1)
    take(0)
    give(2)
    take(1)
    take(2)
    send("rows", "all", input_grad.at[h], input_grad.at[h], sibling)

    def pass_on(n):
        block = piece_of(flip(h, 2), n)
        arrived(("i", n), block)
        if n < len(PIECES) - 1:
            send("rows", "all", block, block, sibling)

    arrived("ay", activations.at[flip(h, 2)])
    send("rows", "all", activations.at[flip(h, 2)], activations.at[flip(h, 2)], sibling)
    arrived("g", grads_in)
    grads_all[part] = grads[0] + grads_in[...]
    for peer in (x_peer, z_peer, xz_peer):
        send("g", "sums", grads_all.at[part], grads_all.at[part], peer)
    pass_on(0)
    arrived("sums", grads_all.at[pl.ds(0, 3)])
    sums = (grads_all[0] + grads_all[1]) + (grads_all[2] + grads_all[3])
    for n, peer in enumerate(batch_peers):
        grads_sums[2 * n] = sums
        send("g", ("g", n), grads_sums.at[2 * n], grads_sums.at[2 * n + 1], peer)
        if n == 0:
            for m in range(1, len(PIECES)):
                pass_on(m)
        arrived(("g", n), grads_sums.at[2 * n + 1])
        sums = sums + grads_sums[2 * n + 1]
    grads_out[...] = sums
    for n in range(1, 1 if batch_peers else len(PIECES)):
        pass_on(n)
    arrived("all", activations)

    def rows_block(count):
        tiles = count // 16
        shapes = [(m, n, tiles // (m * n)) for m in (1, 2, 3, 4) for n in range(1, 13) if tiles % (m * n) == 0]
        inner, outer, depth = next(shape for shape in shapes if shape[2] <= 12)
        return w.at[pl.ds(0, inner), pl.ds(0, outer), pl.ds(0, 16 * depth)]

    sent("y", w.at[FAR, pl.ds(0, 3)])
    sent("x", rows_block(48 * ITEMS + 24 * len(TWICE)))
    sent("z", rows_block(48 * ITEMS + 24 * len(TWICE)))
    sent("t", rows_block(sum(OVER_Y)))
    sent("d", rows_block(sum(48 - OVER_Y[n] for n in range(ITEMS) if n not in TWICE)))
    sent("c", w.at[FAR, pl.ds(0, 9)])
    sent("w", w.at[SIB, pl.ds(0, 9)])
    sent("ctx", ctx_in.at[pl.ds(0, 3)])
    sent("dctx", dctx_in.at[0])
    sent("rows", w.at[pl.ds(0, 4), pl.ds(0, 7), pl.ds(0, 64)])
    sent("b", ups_out.at[0])
    sent("l", log_sum.at[0])
    sent("g", grads_sums.at[pl.ds(0, 4 + len(batch_peers))])


def hand_over(activations, input_grad, grads, *rest):
    targets, sem = rest[:4], rest[4]
    sources = (activations, input_grad, grads.at[0], grads.at[1])
    copies = [
        pltpu.make_async_copy(source, target, sem.at[n])
        for n, (source, target) in enumerate(zip(sources, targets))
    ]
    for c in copies:
        c.start()
    for c in copies:
        c.wait()


def body(batch, *given):
    (
        tokens,
        lengths,
        w_query,
        w_key,
        w_value,
        w_out,
        down_query,
        down_value,
        up_query,
        up_value,
        w_up,
        w_down,
        gain_attn,
        gain_ffn,
        cotangent,
    ) = given
    anywhere = pl.BlockSpec(memory_space=pl.ANY)
    in_vmem = pl.BlockSpec(memory_space=pltpu.VMEM)
    in_hbm = pl.BlockSpec(memory_space=pltpu.HBM)
    vmem = pltpu.VMEM
    results = pl.pallas_call(
        functools.partial(kernel, batch),
        out_shape=(
            vmem((4, 256, 768), BF16),
            vmem((4, 256, 768), BF16),
            vmem((2, 8, 192), F32),
        ),
        in_specs=[pl.BlockSpec(memory_space=pltpu.SMEM)] + [in_hbm] * 14,
        out_specs=(in_vmem,) * 3,
        scratch_shapes=[
            vmem((4, 256, 768), BF16),
            vmem((4, 13, 192, 768), BF16),
            vmem((2, 8, 768), BF16),
            vmem((2, 8, 192), BF16),
            vmem((2, 768), F32),
            vmem((256, 768), BF16),
            vmem((2, 16, 576), F32),
            vmem((2, 16, 192), BF16),
            vmem((16, 512), BF16),
            vmem((2, 576, 512), BF16),
            vmem((2, 3, 512, 512), BF16),
            vmem((2, 3, 1, 512), F32),
            vmem((2, 2, 192, 256), BF16),
            vmem((4, 192, 256), BF16),
            vmem((256, 768), F32),
            vmem((256, 1), F32),
            vmem((256, 768), F32),
            vmem((256, 768), BF16),
            vmem((4, 256, 768), BF16),
            vmem((4, 256, 768), F32),
            vmem((256, 768), F32),
            vmem((256, 768), F32),
            vmem((2, 256, 768), F32),
            vmem((4, 192, 256), BF16),
            vmem((2, 2, 192, 256), BF16),
            vmem((2, 608, 512), BF16),
            vmem((256, 768), BF16),
            vmem((256, 768), BF16),
            vmem((2, 2, 8, 192), F32),
            vmem((2, 8, 192), F32),
            vmem((4, 2, 8, 192), F32),
            vmem((2 * batch.bit_length(), 2, 8, 192), F32),
            pltpu.SemaphoreType.DMA((9,)),
            pltpu.SemaphoreType.DMA((len(SEND_GROUPS),)),
            pltpu.SemaphoreType.DMA((34 + 2 * len(TWICE) + batch.bit_length() + len(SPANS) + len(PIECES),)),
        ],
        compiler_params=pltpu.CompilerParams(
            collective_id=0, has_side_effects=True, vmem_limit_bytes=56 * 1024 * 1024
        ),
        cost_estimate=pl.CostEstimate(
            flops=11_000_000_000, bytes_accessed=20_000_000, transcendentals=4_000_000
        ),
    )(
        lengths,
        tokens.reshape(4, 256, 768),
        w_query.T,
        w_key.T,
        w_value.T,
        w_out.reshape(1, 192, 768),
        w_up.reshape(4, 192, 768),
        w_down.reshape(4, 192, 768),
        down_query.T,
        down_value.T,
        up_query,
        up_value,
        gain_attn,
        gain_ffn,
        cotangent.reshape(4, 256, 768),
    )
    rows = jax.ShapeDtypeStruct((4, 256, 768), BF16)
    small = jax.ShapeDtypeStruct((8, 192), F32)
    activations, input_grad, grad_b_query, grad_b_value = pl.pallas_call(
        hand_over,
        out_shape=(rows, rows, small, small),
        in_specs=[anywhere] * 3,
        out_specs=[in_hbm] * 4,
        scratch_shapes=[pltpu.SemaphoreType.DMA((4,))],
        compiler_params=pltpu.CompilerParams(vmem_limit_bytes=1024 * 1024),
    )(*results)
    return (
        activations.reshape(tokens.shape),
        input_grad.reshape(tokens.shape),
        grad_b_query,
        grad_b_value,
    )


def solution(mesh):
    batch = mesh.shape["batch"]
    in_specs = (
        P("batch", None),
        P("batch"),
        P(None, "head"),
        P(None, "head"),
        P(None, "head"),
        P("head", None),
        P(),
        P(),
        P(None, "head"),
        P(None, "head"),
        P(None, "head"),
        P("head", None),
        P(),
        P(),
        P("batch", None),
    )
    out_specs = (P("batch", None), P("batch", None), P(None, "head"), P(None, "head"))
    return jax.shard_map(
        functools.partial(body, batch),
        mesh=mesh,
        in_specs=in_specs,
        out_specs=out_specs,
        check_vma=False,
    )
```
